512 devices in a mesh: cells: 64 (over z, x), days: 8 (over y, core).
Axes of the slice: x: 4, y: 4, z: 16, core: 2. Of those that a mesh axis runs over, the one named last changes fastest.
Arguments:
- field: float32 [2048, 262144], P('days', 'cells'), may hold values from -600 to 600, as said below
- pcs: float32 [100, 2048], P(None, 'days'), may hold values from -6 to 6
Outputs:
- rotated_loadings: float32 [100, 262144], P(None, ('cells', 'days'))
- series: float32 [100, 2048], P(None, 'days')
The draws below stay inside these ranges and needn't reach their ends.
Inputs may be any that keep to these rules, and one draw needn't show every extreme that they name: `field`: each entry is a day factor times a cell factor times a bounded random value.
All inputs are finite; a program needn't handle non-finite values.
Results may differ from the reference program's by a relative error of at most 0.00022.
Values sent between devices are 32-bit elements; how exact they have to be, the bound alone decides.
No kernel may reach another device: no remote copies, remote signals or barrier semaphores. Data moves between devices by JAX's collectives and lax.ppermute only.
A program may use at most 64 MiB of HBM per device.

```python
import math
import jax
import jax.numpy as jnp
from jax import lax

K = 100
ITERS = 3
NS_STEPS = 12
CELLS = 262144
DAYS = 2048


def draw_field(key, part):
    key = jax.random.fold_in(key, 1)
    k_cell, k_day, k_val = jax.random.split(key, 3)
    cell_scale = jnp.exp(jax.random.uniform(k_cell, (1, CELLS), jnp.float32) * math.log(10.0))
    day_scale = jnp.exp(jax.random.uniform(k_day, (DAYS, 1), jnp.float32) * math.log(10.0))
    values = jnp.clip(jax.random.normal(k_val, (DAYS, CELLS), jnp.float32), -6.0, 6.0)
    return values * cell_scale * day_scale


def block_levels(stream_key, shape, shards, smallest, largest):
    loudness, own = 1.0, jax.random.fold_in(stream_key, 6)
    for dim, parts in shards:
        heights = jnp.exp(jax.random.uniform(jax.random.fold_in(own, dim), (parts,), jnp.float32, smallest / len(shards), largest / len(shards)))
        loudness = loudness * jnp.repeat(heights, shape[dim] // parts).reshape([-1 if axis == dim else 1 for axis in range(len(shape))])
    return loudness


def bell_draw(stream_key, extent, spread, limit, pieces=(), held_as=jnp.bfloat16):
    result = spread * jax.random.normal(stream_key, extent, jnp.float32)
    if pieces:
        result = result * block_levels(stream_key, extent, pieces, -0.22, 0.18)
    return jnp.clip(result, -limit, limit).astype(held_as)


def setup_inputs(seed: int = 0) -> dict:
    arg_keys = jax.random.split(jax.random.key(seed), 3)
    return {
        "field": draw_field(jax.random.fold_in(arg_keys[2], 71), 0),
        "pcs": bell_draw(arg_keys[1], (K, DAYS), 1.0, 6.0, ((1, 8),), jnp.float32),
    }


HIGH = lax.Precision.HIGHEST

def rows_dot(left, right):
    return lax.dot_general(left, right, (((1,), (1,)), ((), ())), precision=HIGH, preferred_element_type=jnp.float32)

def polar(grad):
    x = grad / (jnp.sqrt(jnp.sum(grad * grad)) + 1e-06)
    for step in range(NS_STEPS):
        inner = jnp.dot(x.T, x, precision=HIGH)
        x = 1.5 * x - 0.5 * jnp.dot(x, inner, precision=HIGH)
    return x

def reference(field, pcs):
    loadings = jnp.dot(pcs, field, precision=HIGH) * (1.0 / DAYS ** 0.5)
    rotation = jnp.eye(K, dtype=jnp.float32)
    for step in range(ITERS):
        turned = jnp.dot(rotation.T, loadings, precision=HIGH)
        cube = rows_dot(loadings, turned * turned * turned)
        cross = rows_dot(loadings, turned)
        colsq = lax.optimization_barrier(jnp.sum(turned * turned, axis=1))
        grad = cube - cross * colsq[None, :] / CELLS
        rotation = polar(grad)
    rotated_loadings = jnp.dot(rotation.T, loadings, precision=HIGH)
    series = rows_dot(rotated_loadings, field) * (DAYS ** 0.5 / CELLS)
    return (rotated_loadings, series)
```

```python
import jax
import jax.numpy as jnp
from jax import lax
from jax.sharding import Mesh, PartitionSpec as P

ITERS = 3
NS_STEPS = 12
Z, X, Y, CORE = 16, 4, 4, 2
PLANE = ("x", "y", "core")
DAY = ("y", "core")
PAD = 128
N_PLANE = X * Y * CORE
ROWS = PAD // N_PLANE

HIGH = lax.Precision.HIGH


def dot(left, right):
    return jnp.dot(left, right, precision=HIGH, preferred_element_type=jnp.float32)


def rows_dot(left, right):
    return lax.dot_general(
        left, right, (((1,), (1,)), ((), ())), precision=HIGH, preferred_element_type=jnp.float32
    )


def cols_dot(left, right):
    return lax.dot_general(
        left, right, (((0,), (0,)), ((), ())), precision=HIGH, preferred_element_type=jnp.float32
    )


def polar(grad):
    x = grad / (jnp.sqrt(jnp.sum(grad * grad)) + 1e-06)
    for step in range(NS_STEPS):
        inner = cols_dot(x, x)
        x = 1.5 * x - 0.5 * dot(x, inner)
    return x


def swap(value, axes):
    return lax.all_to_all(value, axes, 0, 0)


def spread(value, count):
    return jnp.broadcast_to(value, (count,) + value.shape)


def plane_scatter(terms):
    k = terms[0].shape[0]
    padded = [jnp.pad(t, ((0, PAD - k), (0, PAD - k))).reshape(N_PLANE, ROWS, PAD) for t in terms]
    return jnp.sum(swap(jnp.concatenate(padded, axis=1), PLANE), axis=0)


def on_device(field, pcs):
    k, days_here = pcs.shape
    groups = Y * CORE
    days_total = days_here * groups
    share = field.shape[1] // groups
    cells_total = field.shape[1] * Z * X
    parts = jnp.stack([dot(pcs, field[:, g * share : (g + 1) * share]) for g in range(groups)])
    loadings = jnp.sum(swap(parts, DAY), axis=0) * (1.0 / days_total**0.5)

    every = lax.all_gather(loadings, DAY)

    cubed = loadings * loadings * loadings
    chunk = plane_scatter([rows_dot(loadings, cubed), rows_dot(loadings, loadings)])
    chunk = jnp.sum(swap(spread(chunk, Z), "z"), axis=0)
    got = swap(spread(chunk, N_PLANE), PLANE)
    cube = got[:, :ROWS].reshape(PAD, PAD)[:k, :k]
    corr = got[:, ROWS:].reshape(PAD, PAD)[:k, :k]
    colsq = jnp.sum(jnp.eye(k, dtype=jnp.float32) * corr, axis=0)
    rotation = polar(cube - corr * colsq[None, :] / cells_total)

    terms = sum(
        lax.dot_general(
            field[:, g * share : (g + 1) * share],
            every[g],
            (((1,), (1,)), ((), ())),
            precision=HIGH,
            preferred_element_type=jnp.float32,
        )
        for g in range(groups)
    ) * (days_total**0.5 / cells_total)
    piece = days_here // Z
    terms = jnp.pad(terms, ((0, 0), (0, PAD - k))).reshape(Z, piece, PAD)

    turned = cols_dot(rotation, loadings)
    chunk = plane_scatter([rows_dot(loadings, turned * turned * turned)])
    sent = jnp.concatenate([spread(chunk, Z), terms], axis=1)
    chunk = jnp.sum(swap(sent, "z"), axis=0)
    got = swap(spread(chunk, N_PLANE), PLANE)
    cube = got[:, :ROWS].reshape(PAD, PAD)[:k, :k]
    mine = lax.axis_index(DAY)
    terms = got[:, ROWS:].reshape(X, groups, piece, PAD)
    terms = jnp.sum(lax.dynamic_index_in_dim(terms, mine, 1, keepdims=False), axis=0)
    cross = dot(corr, rotation)
    colsq = jnp.sum(rotation * cross, axis=0)
    rotation = polar(cube - cross * colsq[None, :] / cells_total)

    turned = cols_dot(rotation, loadings)
    chunk = plane_scatter([rows_dot(loadings, turned * turned * turned)])
    got = swap(spread(jnp.concatenate([chunk, terms], axis=0), Z), "z")
    terms = got[:, ROWS:].reshape(days_here, PAD)[:, :k]
    chunk = jnp.sum(got[:, :ROWS], axis=0)
    got = swap(spread(chunk, N_PLANE), PLANE)
    cube = got.reshape(PAD, PAD)[:k, :k]
    cross = dot(corr, rotation)
    colsq = jnp.sum(rotation * cross, axis=0)
    rotation = polar(cube - cross * colsq[None, :] / cells_total)

    series = lax.dot_general(
        rotation, terms, (((0,), (1,)), ((), ())), precision=HIGH, preferred_element_type=jnp.float32
    )
    return (cols_dot(rotation, loadings), series)


def solution(mesh):
    split = Mesh(mesh.devices.reshape(Z, X, Y, CORE), ("z", "x", "y", "core"))
    placed = (P(DAY, ("z", "x")), P(None, DAY))
    return jax.shard_map(
        on_device,
        mesh=split,
        in_specs=placed,
        out_specs=(P(None, ("z", "x", "y", "core")), P(None, DAY)),
        check_vma=False,
    )
```

```python
import functools

import jax
import jax.numpy as jnp
from jax import lax
from jax.experimental import pallas as pl
from jax.experimental.pallas import tpu as pltpu
from jax.sharding import Mesh, PartitionSpec as P

ITERS = 3
NS_STEPS = 12
Z, X, Y, CORE = 16, 4, 4, 2
PLANE = ("x", "y", "core")
DAY = ("y", "core")
PAD = 128
N_PLANE = X * Y * CORE
ROWS = PAD // N_PLANE
F32 = jnp.float32
VMEM = pl.BlockSpec(memory_space=pltpu.VMEM)
LIMIT = 16 << 20
WIDE_LIMIT = 60 << 20


def split(value):
    high = value.astype(jnp.bfloat16)
    return high, (value - high.astype(F32)).astype(jnp.bfloat16)


def nn(left, right):
    return jnp.dot(left, right, preferred_element_type=F32)


def nt(left, right):
    return lax.dot_general(left, right, (((1,), (1,)), ((), ())), preferred_element_type=F32)


def fold(value):
    half = value.shape[1] // 2
    return value[:, :half] + value[:, half:]


def pad_rows(value, rows):
    return jnp.concatenate([value, jnp.zeros((rows - value.shape[0], value.shape[1]), F32)], axis=0)


def small_nn(left, right):
    lh, ll = split(left)
    rh, rl = split(right)
    both = jnp.concatenate([rh, rl], axis=1)
    return fold(nn(jnp.concatenate([lh, ll], axis=1), jnp.concatenate([both, both], axis=0)))


def rows_nt(left, right):
    lh, ll = split(left)
    rh, rl = split(right)
    return fold(nt(lh, jnp.concatenate([rh, rl], axis=0))) + nt(ll, rh)


def polar_rows(grad):
    norm = jnp.sqrt(jnp.sum(jnp.sum(grad * grad, axis=1, keepdims=True), axis=0, keepdims=True))
    y = grad / (norm + 1e-06)
    for step in range(NS_STEPS):
        high, low = split(y)
        down = jnp.concatenate([high, low], axis=0)
        across = jnp.concatenate([high, low], axis=1)
        inner = fold(nt(across, jnp.concatenate([down, down], axis=1)))
        ih, il = split(inner)
        again = jnp.concatenate([across, across], axis=0)
        y = 1.5 * y - 0.5 * fold(nn(jnp.concatenate([ih, il], axis=1), again))
    return y


def turn_cube(y, loadings):
    turned = small_nn(y, loadings)
    return rows_nt(turned * turned * turned, loadings)


def parts_kernel(scale, where_ref, pcs_ref, field_ref, out_ref, wide, left):
    half = wide.shape[0]

    @pl.when(pl.program_id(0) == 0)
    def _():
        wide[...] = jnp.zeros_like(wide)
        wide[0 : pcs_ref.shape[0]] = pcs_ref[...]
        high, low = split(wide[...])
        left[0:half] = high
        left[half : 2 * half] = low

    high, low = split(field_ref[...])
    both = nn(left[...], high)
    total = both[0:half] + both[half : 2 * half] + nn(left[0:half], low)
    out_ref[0] = total[0 : out_ref.shape[1]] * scale


def parts(field, pcs, core, scale):
    k, days = pcs.shape
    share = field.shape[1] // (Y * CORE)
    half = (k + 15) // 16 * 16
    rows = (k + 7) // 8 * 8
    return pl.pallas_call(
        functools.partial(parts_kernel, scale),
        out_shape=jax.ShapeDtypeStruct((Y, rows, share), F32),
        grid_spec=pltpu.PrefetchScalarGridSpec(
            num_scalar_prefetch=1,
            grid=(Y,),
            in_specs=[
                pl.BlockSpec((k, days), lambda g, where: (0, 0)),
                pl.BlockSpec((days, share), lambda g, where: (0, CORE * g + where[0])),
            ],
            out_specs=pl.BlockSpec((1, rows, share), lambda g, where: (g, 0, 0)),
            scratch_shapes=[pltpu.VMEM((half, days), F32), pltpu.VMEM((2 * half, days), jnp.bfloat16)],
        ),
        cost_estimate=pl.CostEstimate(
            flops=6 * k * days * share * Y, bytes_accessed=4 * Y * share * (days + k), transcendentals=0
        ),
        compiler_params=pltpu.CompilerParams(vmem_limit_bytes=WIDE_LIMIT),
    )(core, pcs, field)


def first_kernel(recv_ref, sent_ref, loadings_ref, padded_ref):
    loadings = recv_ref[0] + recv_ref[1] + recv_ref[2] + recv_ref[3]
    k = loadings.shape[0]
    padded_ref[...] = jnp.zeros_like(padded_ref)
    padded_ref[0:k] = loadings
    loadings_ref[...] = loadings
    loadings = padded_ref[...]
    sent_ref[0:PAD] = rows_nt(loadings * loadings * loadings, loadings)
    sent_ref[PAD : 2 * PAD] = rows_nt(loadings, loadings)


def first(recv):
    k, share = recv.shape[1:]
    return pl.pallas_call(
        first_kernel,
        out_shape=(
            jax.ShapeDtypeStruct((2 * PAD, PAD), F32),
            jax.ShapeDtypeStruct((k, share), F32),
            jax.ShapeDtypeStruct((PAD, share), F32),
        ),
        in_specs=[VMEM],
        out_specs=(VMEM, VMEM, VMEM),
        compiler_params=pltpu.CompilerParams(vmem_limit_bytes=LIMIT),
    )(recv)


def second_kernel(cells, got_ref, loadings_ref, sent_ref, y_ref):
    corr = got_ref[PAD : 2 * PAD]
    rows = lax.broadcasted_iota(jnp.int32, corr.shape, 0)
    columns = lax.broadcasted_iota(jnp.int32, corr.shape, 1)
    colsq = jnp.sum(jnp.where(rows == columns, corr, 0.0), axis=1, keepdims=True)
    y = polar_rows(got_ref[0:PAD] - corr * colsq * (1.0 / cells))
    y_ref[...] = y
    sent_ref[...] = turn_cube(y, loadings_ref[...])


def next_y(cells, cube_ref, got_ref, y_ref):
    y = y_ref[...]
    cross = small_nn(y, got_ref[PAD : 2 * PAD])
    colsq = jnp.sum(y * cross, axis=1, keepdims=True)
    return polar_rows(cube_ref[...] - cross * colsq * (1.0 / cells))


def third_kernel(cells, cube_ref, got_ref, y_ref, loadings_ref, sent_ref, out_ref):
    y = next_y(cells, cube_ref, got_ref, y_ref)
    out_ref[...] = y
    sent_ref[...] = turn_cube(y, loadings_ref[...])


def last_kernel(cells, cube_ref, got_ref, y_ref, loadings_ref, terms_ref, rotated_ref, series_ref):
    k = rotated_ref.shape[0]
    y = next_y(cells, cube_ref, got_ref, y_ref)
    rotated_ref[...] = small_nn(y, loadings_ref[...])[0:k]
    series_ref[...] = rows_nt(y, terms_ref[...])[0:k]


def whole(kernel, outs, *args):
    return pl.pallas_call(
        kernel,
        out_shape=tuple(jax.ShapeDtypeStruct(s, F32) for s in outs),
        in_specs=[VMEM] * len(args),
        out_specs=(VMEM,) * len(outs),
        compiler_params=pltpu.CompilerParams(vmem_limit_bytes=LIMIT),
    )(*args)


def terms_kernel(scale, where_ref, mine_ref, other_ref, near_ref, far_ref, out_ref):
    def product(field, loadings):
        high, low = split(field)
        lh, ll = split(pad_rows(loadings, PAD))
        return fold(nt(high, jnp.concatenate([lh, ll], axis=0))) + nt(low, lh)

    total = product(mine_ref[...], near_ref[0]) + product(other_ref[...], far_ref[0])
    g = pl.program_id(0)

    @pl.when(g == 0)
    def _():
        out_ref[...] = total * scale

    @pl.when(g > 0)
    def _():
        out_ref[...] += total * scale


def series_terms(field, near, far, where, scale):
    days = field.shape[0]
    rows, share = near.shape[1:]
    mine = lambda d, where: (0, lax.rem(where[0] + Y - d, Y) * CORE + where[1])
    other = lambda d, where: (0, lax.rem(where[0] + Y - d, Y) * CORE + 1 - where[1])
    return pl.pallas_call(
        functools.partial(terms_kernel, scale),
        out_shape=jax.ShapeDtypeStruct((days, PAD), F32),
        grid_spec=pltpu.PrefetchScalarGridSpec(
            num_scalar_prefetch=1,
            grid=(Y,),
            in_specs=[
                pl.BlockSpec((days, share), mine),
                pl.BlockSpec((days, share), other),
                pl.BlockSpec((1, rows, share), lambda d, where: (d, 0, 0)),
                pl.BlockSpec((1, rows, share), lambda d, where: (d, 0, 0)),
            ],
            out_specs=pl.BlockSpec((days, PAD), lambda d, where: (0, 0)),
        ),
        cost_estimate=pl.CostEstimate(
            flops=6 * days * PAD * share * Y * CORE,
            bytes_accessed=4 * Y * CORE * share * (days + rows),
            transcendentals=0,
        ),
        compiler_params=pltpu.CompilerParams(vmem_limit_bytes=WIDE_LIMIT),
    )(where, field, field, near, far)


def swap(value, axes):
    return lax.all_to_all(value, axes, 0, 0)


def spread(value, count):
    return jnp.broadcast_to(value, (count,) + value.shape)


def on_device(field, pcs):
    k, days_here = pcs.shape
    groups = Y * CORE
    days_total = days_here * groups
    cells_total = field.shape[1] * Z * X
    share = field.shape[1] // groups
    core = lax.axis_index("core").astype(jnp.int32)
    row = lax.axis_index("y").astype(jnp.int32)

    scale = 1.0 / days_total**0.5
    theirs = lax.ppermute(parts(field, pcs, (1 - core)[None], scale), "core", [(0, 1), (1, 0)])
    recv = swap(theirs + parts(field, pcs, core[None], scale), "y")
    sent, narrow, loadings = first(recv)

    chunk = swap(sent.reshape(N_PLANE, 2 * ROWS, PAD), PLANE)
    near = [lax.ppermute(narrow, "y", [(i, (i + d) % Y) for i in range(Y)]) for d in range(1, Y)]
    chunk, near = lax.optimization_barrier((chunk, near))
    near = jnp.stack([narrow] + near)
    far = lax.ppermute(near, "core", [(0, 1), (1, 0)])
    chunk = swap(spread(jnp.sum(chunk, axis=0), Z), "z")
    chunk, near, far = lax.optimization_barrier((chunk, near, far))
    terms = series_terms(field, near, far, jnp.stack([row, core]), days_total**0.5 / cells_total)
    base = swap(spread(jnp.sum(chunk, axis=0), N_PLANE), PLANE)
    base, terms = lax.optimization_barrier((base, terms))
    base = base.reshape(2 * PAD, PAD)
    piece = days_here // Z
    sent, y = whole(functools.partial(second_kernel, cells_total), [(PAD, PAD)] * 2, base, loadings)

    chunk = jnp.sum(swap(sent.reshape(N_PLANE, ROWS, PAD), PLANE), axis=0)
    both = jnp.concatenate([spread(chunk, Z), terms.reshape(Z, piece, PAD)], axis=1)
    both = jnp.sum(swap(both, "z"), axis=0)
    got = swap(spread(both, N_PLANE), PLANE)
    cube = got[:, :ROWS].reshape(PAD, PAD)
    terms = got[:, ROWS:].reshape(X, groups, piece, PAD)
    terms = jnp.sum(lax.dynamic_index_in_dim(terms, row * CORE + core, 1, keepdims=False), axis=0)
    sent, y = whole(
        functools.partial(third_kernel, cells_total), [(PAD, PAD)] * 2, cube, base, y, loadings
    )

    chunk = jnp.sum(swap(sent.reshape(N_PLANE, ROWS, PAD), PLANE), axis=0)
    got = swap(spread(jnp.concatenate([chunk, terms], axis=0), Z), "z")
    terms = got[:, ROWS:].reshape(days_here, PAD)
    chunk = jnp.sum(got[:, :ROWS], axis=0)
    cube = swap(spread(chunk, N_PLANE), PLANE).reshape(PAD, PAD)
    return whole(
        functools.partial(last_kernel, cells_total),
        [(k, share), (k, days_here)],
        cube, base, y, loadings, terms,
    )


def solution(mesh):
    split_mesh = Mesh(mesh.devices.reshape(Z, X, Y, CORE), ("z", "x", "y", "core"))
    placed = (P(DAY, ("z", "x")), P(None, DAY))
    return jax.shard_map(
        on_device,
        mesh=split_mesh,
        in_specs=placed,
        out_specs=(P(None, ("z", "x", "y", "core")), P(None, DAY)),
        check_vma=False,
    )
```

```python
import functools

import jax
import jax.numpy as jnp
from jax import lax
from jax.experimental import pallas as pl
from jax.experimental.pallas import tpu as pltpu
from jax.sharding import Mesh, PartitionSpec as P

ITERS = 3
NS_STEPS = 12
Z, X, Y, CORE = 16, 4, 4, 2
PLANE = ("x", "y", "core")
DAY = ("y", "core")
PAD = 128
N_PLANE = X * Y * CORE
ROWS = PAD // N_PLANE
F32 = jnp.float32
VMEM = pl.BlockSpec(memory_space=pltpu.VMEM)
LIMIT = 24 << 20


def split(value):
    high = value.astype(jnp.bfloat16)
    return high, (value - high.astype(F32)).astype(jnp.bfloat16)


def nn(left, right):
    return jnp.dot(left, right, preferred_element_type=F32)


def nt(left, right):
    return lax.dot_general(left, right, (((1,), (1,)), ((), ())), preferred_element_type=F32)


def fold(value):
    half = value.shape[1] // 2
    return value[:, :half] + value[:, half:]


def pad_rows(value, rows):
    return jnp.concatenate([value, jnp.zeros((rows - value.shape[0], value.shape[1]), F32)], axis=0)


def small_nn(left, right):
    lh, ll = split(left)
    rh, rl = split(right)
    both = jnp.concatenate([rh, rl], axis=1)
    return fold(nn(jnp.concatenate([lh, ll], axis=1), jnp.concatenate([both, both], axis=0)))


def rows_nt(left, right):
    lh, ll = split(left)
    rh, rl = split(right)
    return fold(nt(lh, jnp.concatenate([rh, rl], axis=0))) + nt(ll, rh)


def polar_rows(grad):
    norm = jnp.sqrt(jnp.sum(jnp.sum(grad * grad, axis=1, keepdims=True), axis=0, keepdims=True))
    y = grad / (norm + 1e-06)
    for step in range(NS_STEPS):
        high, low = split(y)
        down = jnp.concatenate([high, low], axis=0)
        across = jnp.concatenate([high, low], axis=1)
        inner = fold(nt(across, jnp.concatenate([down, down], axis=1)))
        ih, il = split(inner)
        again = jnp.concatenate([across, across], axis=0)
        y = 1.5 * y - 0.5 * fold(nn(jnp.concatenate([ih, il], axis=1), again))
    return y


def turn_cube(y, loadings):
    turned = small_nn(y, loadings)
    return rows_nt(turned * turned * turned, loadings)


def columns(field_ref, group, share):
    return field_ref[:, pl.ds(pl.multiple_of(group * share, share), share)]


def parts_kernel(scale, core_ref, pcs_ref, field_ref, out_ref, wide):
    wide[...] = jnp.zeros_like(wide)
    wide[0 : pcs_ref.shape[0]] = pcs_ref[...] * scale
    half = wide.shape[0]
    left_high, left_low = split(wide[...])
    left = jnp.concatenate([left_high, left_low], axis=0)
    for g in range(Y):
        high, low = split(columns(field_ref, CORE * g + core_ref[0], out_ref.shape[2]))
        both = nn(left, high)
        total = both[0:half] + both[half : 2 * half] + nn(left_high, low)
        out_ref[g] = total[0 : out_ref.shape[1]]


def parts(field, pcs, core, scale):
    k, days = pcs.shape
    share = field.shape[1] // (Y * CORE)
    half = (k + 15) // 16 * 16
    rows = (k + 7) // 8 * 8
    return pl.pallas_call(
        functools.partial(parts_kernel, scale),
        out_shape=jax.ShapeDtypeStruct((Y, rows, share), F32),
        in_specs=[pl.BlockSpec(memory_space=pltpu.SMEM), VMEM, VMEM],
        out_specs=VMEM,
        scratch_shapes=[pltpu.VMEM((half, days), F32)],
        cost_estimate=pl.CostEstimate(
            flops=6 * k * days * share * Y, bytes_accessed=4 * Y * share * (days + k), transcendentals=0
        ),
        compiler_params=pltpu.CompilerParams(vmem_limit_bytes=LIMIT),
    )(core, pcs, field)


def first_kernel(recv_ref, sent_ref, loadings_ref, padded_ref):
    loadings = recv_ref[0] + recv_ref[1] + recv_ref[2] + recv_ref[3]
    k = loadings.shape[0]
    padded_ref[...] = jnp.zeros_like(padded_ref)
    padded_ref[0:k] = loadings
    loadings_ref[...] = loadings
    loadings = padded_ref[...]
    sent_ref[0:PAD] = rows_nt(loadings * loadings * loadings, loadings)
    sent_ref[PAD : 2 * PAD] = rows_nt(loadings, loadings)


def first(recv):
    k, share = recv.shape[1:]
    return pl.pallas_call(
        first_kernel,
        out_shape=(
            jax.ShapeDtypeStruct((2 * PAD, PAD), F32),
            jax.ShapeDtypeStruct((k, share), F32),
            jax.ShapeDtypeStruct((PAD, share), F32),
        ),
        in_specs=[VMEM],
        out_specs=(VMEM, VMEM, VMEM),
        compiler_params=pltpu.CompilerParams(vmem_limit_bytes=LIMIT),
    )(recv)


def second_kernel(cells, got_ref, loadings_ref, sent_ref, y_ref):
    corr = got_ref[PAD : 2 * PAD]
    rows = lax.broadcasted_iota(jnp.int32, corr.shape, 0)
    columns = lax.broadcasted_iota(jnp.int32, corr.shape, 1)
    colsq = jnp.sum(jnp.where(rows == columns, corr, 0.0), axis=1, keepdims=True)
    y = polar_rows(got_ref[0:PAD] - corr * colsq * (1.0 / cells))
    y_ref[...] = y
    sent_ref[...] = turn_cube(y, loadings_ref[...])


def next_y(cells, cube_ref, got_ref, y_ref):
    y = y_ref[...]
    cross = small_nn(y, got_ref[PAD : 2 * PAD])
    colsq = jnp.sum(y * cross, axis=1, keepdims=True)
    return polar_rows(cube_ref[...] - cross * colsq * (1.0 / cells))


def third_kernel(cells, cube_ref, got_ref, y_ref, loadings_ref, sent_ref, out_ref):
    y = next_y(cells, cube_ref, got_ref, y_ref)
    out_ref[...] = y
    sent_ref[...] = turn_cube(y, loadings_ref[...])


def last_kernel(cells, cube_ref, got_ref, y_ref, loadings_ref, terms_ref, rotated_ref, series_ref):
    k = rotated_ref.shape[0]
    y = next_y(cells, cube_ref, got_ref, y_ref)
    rotated_ref[...] = small_nn(y, loadings_ref[...])[0:k]
    series_ref[...] = rows_nt(y, terms_ref[...])[0:k]


def whole(kernel, outs, *args):
    return pl.pallas_call(
        kernel,
        out_shape=tuple(jax.ShapeDtypeStruct(s, F32) for s in outs),
        in_specs=[VMEM] * len(args),
        out_specs=(VMEM,) * len(outs),
        compiler_params=pltpu.CompilerParams(vmem_limit_bytes=LIMIT),
    )(*args)


def terms_kernel(scale, where_ref, field_ref, near_ref, far_ref, out_ref):
    row, core = where_ref[0], where_ref[1]
    share = near_ref.shape[2]
    total = jnp.zeros(out_ref.shape, F32)
    for d in range(Y):
        group = CORE * lax.rem(row + Y - d, Y)
        for owner, loadings in ((core, near_ref[d]), (1 - core, far_ref[d])):
            lh, ll = split(pad_rows(loadings, PAD))
            high, low = split(columns(field_ref, group + owner, share))
            total += fold(nt(high, jnp.concatenate([lh, ll], axis=0))) + nt(low, lh)
    out_ref[...] = total * scale


def series_terms(field, near, far, where, scale):
    days = field.shape[0]
    rows, share = near.shape[1:]
    return pl.pallas_call(
        functools.partial(terms_kernel, scale),
        out_shape=jax.ShapeDtypeStruct((days, PAD), F32),
        in_specs=[pl.BlockSpec(memory_space=pltpu.SMEM), VMEM, VMEM, VMEM],
        out_specs=VMEM,
        cost_estimate=pl.CostEstimate(
            flops=6 * days * PAD * share * Y * CORE,
            bytes_accessed=4 * Y * CORE * share * (days + rows),
            transcendentals=0,
        ),
        compiler_params=pltpu.CompilerParams(vmem_limit_bytes=LIMIT),
    )(where, field, near, far)


def swap(value, axes):
    return lax.all_to_all(value, axes, 0, 0)


def spread(value, count):
    return jnp.broadcast_to(value, (count,) + value.shape)


def on_device(field, pcs):
    k, days_here = pcs.shape
    groups = Y * CORE
    days_total = days_here * groups
    cells_total = field.shape[1] * Z * X
    share = field.shape[1] // groups
    core = lax.axis_index("core").astype(jnp.int32)
    row = lax.axis_index("y").astype(jnp.int32)

    scale = 1.0 / days_total**0.5
    theirs = lax.ppermute(parts(field, pcs, (1 - core)[None], scale), "core", [(0, 1), (1, 0)])
    recv = swap(theirs + parts(field, pcs, core[None], scale), "y")
    sent, narrow, loadings = first(recv)

    chunk = swap(sent.reshape(N_PLANE, 2 * ROWS, PAD), PLANE)
    near = [lax.ppermute(narrow, "y", [(i, (i + d) % Y) for i in range(Y)]) for d in range(1, Y)]
    chunk = swap(spread(jnp.sum(chunk, axis=0), Z), "z")
    base = swap(spread(jnp.sum(chunk, axis=0), N_PLANE), PLANE)
    base, near = lax.optimization_barrier((base, near))
    near = jnp.stack([narrow] + near)
    far = lax.ppermute(near, "core", [(0, 1), (1, 0)])
    base = base.reshape(2 * PAD, PAD)
    piece = days_here // Z
    sent, y = whole(functools.partial(second_kernel, cells_total), [(PAD, PAD)] * 2, base, loadings)

    sent, near, far = lax.optimization_barrier((sent, near, far))
    terms = series_terms(field, near, far, jnp.stack([row, core]), days_total**0.5 / cells_total)
    chunk, terms = lax.optimization_barrier((swap(sent.reshape(N_PLANE, ROWS, PAD), PLANE), terms))
    chunk = jnp.sum(chunk, axis=0)
    both = jnp.concatenate([spread(chunk, Z), terms.reshape(Z, piece, PAD)], axis=1)
    both = jnp.sum(swap(both, "z"), axis=0)
    got = swap(spread(both, N_PLANE), PLANE)
    cube = got[:, :ROWS].reshape(PAD, PAD)
    terms = got[:, ROWS:].reshape(X, groups, piece, PAD)
    terms = jnp.sum(lax.dynamic_index_in_dim(terms, row * CORE + core, 1, keepdims=False), axis=0)
    sent, y = whole(
        functools.partial(third_kernel, cells_total), [(PAD, PAD)] * 2, cube, base, y, loadings
    )

    chunk = jnp.sum(swap(sent.reshape(N_PLANE, ROWS, PAD), PLANE), axis=0)
    got = swap(spread(jnp.concatenate([chunk, terms], axis=0), Z), "z")
    terms = got[:, ROWS:].reshape(days_here, PAD)
    chunk = jnp.sum(got[:, :ROWS], axis=0)
    cube = swap(spread(chunk, N_PLANE), PLANE).reshape(PAD, PAD)
    return whole(
        functools.partial(last_kernel, cells_total),
        [(k, share), (k, days_here)],
        cube, base, y, loadings, terms,
    )


def solution(mesh):
    split_mesh = Mesh(mesh.devices.reshape(Z, X, Y, CORE), ("z", "x", "y", "core"))
    placed = (P(DAY, ("z", "x")), P(None, DAY))
    return jax.shard_map(
        on_device,
        mesh=split_mesh,
        in_specs=placed,
        out_specs=(P(None, ("z", "x", "y", "core")), P(None, DAY)),
        check_vma=False,
    )
```

```python
import functools

import jax
import jax.numpy as jnp
from jax import lax
from jax.experimental import pallas as pl
from jax.experimental.pallas import tpu as pltpu
from jax.sharding import Mesh, PartitionSpec as P

ITERS = 3
NS_STEPS = 12
Z, X, Y, CORE = 16, 4, 4, 2
PLANE = ("x", "y", "core")
DAY = ("y", "core")
PAD = 128
N_PLANE = X * Y * CORE
ROWS = PAD // N_PLANE
F32 = jnp.float32
VMEM = pl.BlockSpec(memory_space=pltpu.VMEM)
LIMIT = 24 << 20
WIDE_LIMIT = 52 << 20


def split(value):
    high = value.astype(jnp.bfloat16)
    return high, (value - high.astype(F32)).astype(jnp.bfloat16)


def nn(left, right):
    return jnp.dot(left, right, preferred_element_type=F32)


def nt(left, right):
    return lax.dot_general(left, right, (((1,), (1,)), ((), ())), preferred_element_type=F32)


def fold(value):
    half = value.shape[1] // 2
    return value[:, :half] + value[:, half:]


def pad_rows(value, rows):
    return jnp.concatenate([value, jnp.zeros((rows - value.shape[0], value.shape[1]), F32)], axis=0)


def small_nn(left, right):
    lh, ll = split(left)
    rh, rl = split(right)
    both = jnp.concatenate([rh, rl], axis=1)
    return fold(nn(jnp.concatenate([lh, ll], axis=1), jnp.concatenate([both, both], axis=0)))


def rows_nt(left, right):
    lh, ll = split(left)
    rh, rl = split(right)
    return fold(nt(lh, jnp.concatenate([rh, rl], axis=0))) + nt(ll, rh)


def polar_rows(grad):
    norm = jnp.sqrt(jnp.sum(jnp.sum(grad * grad, axis=1, keepdims=True), axis=0, keepdims=True))
    y = grad / (norm + 1e-06)
    for step in range(NS_STEPS):
        high, low = split(y)
        down = jnp.concatenate([high, low], axis=0)
        across = jnp.concatenate([high, low], axis=1)
        inner = fold(nt(across, jnp.concatenate([down, down], axis=1)))
        ih, il = split(inner)
        again = jnp.concatenate([across, across], axis=0)
        y = 1.5 * y - 0.5 * fold(nn(jnp.concatenate([ih, il], axis=1), again))
    return y


def turn_cube(y, loadings):
    turned = small_nn(y, loadings)
    return rows_nt(turned * turned * turned, loadings)


def columns(field_ref, group, share):
    return field_ref[:, pl.ds(pl.multiple_of(group * share, share), share)]


def parts_kernel(scale, core_ref, pcs_ref, field_ref, out_ref, pcs, wide, field, sems):
    share = out_ref.shape[2]
    copies = [pltpu.make_async_copy(pcs_ref, pcs, sems.at[Y])]
    for g in range(Y):
        start = pl.multiple_of((CORE * g + core_ref[0]) * share, share)
        copies.append(pltpu.make_async_copy(field_ref.at[:, pl.ds(start, share)], field.at[g], sems.at[g]))
    for copy in copies:
        copy.start()
    wide[...] = jnp.zeros_like(wide)
    copies[0].wait()
    wide[0 : pcs.shape[0]] = pcs[...] * scale
    half = wide.shape[0]
    left_high, left_low = split(wide[...])
    left = jnp.concatenate([left_high, left_low], axis=0)
    for g in range(Y):
        copies[1 + g].wait()
        high, low = split(field[g])
        both = nn(left, high)
        total = both[0:half] + both[half : 2 * half] + nn(left_high, low)
        out_ref[g] = total[0 : out_ref.shape[1]]


def parts(field, pcs, core, scale):
    k, days = pcs.shape
    share = field.shape[1] // (Y * CORE)
    half = (k + 15) // 16 * 16
    rows = (k + 7) // 8 * 8
    far = pl.BlockSpec(memory_space=pl.ANY)
    return pl.pallas_call(
        functools.partial(parts_kernel, scale),
        out_shape=jax.ShapeDtypeStruct((Y, rows, share), F32),
        in_specs=[pl.BlockSpec(memory_space=pltpu.SMEM), far, far],
        out_specs=VMEM,
        scratch_shapes=[
            pltpu.VMEM((k, days), F32),
            pltpu.VMEM((half, days), F32),
            pltpu.VMEM((Y, days, share), F32),
            pltpu.SemaphoreType.DMA((Y + 1,)),
        ],
        cost_estimate=pl.CostEstimate(
            flops=6 * k * days * share * Y, bytes_accessed=4 * Y * share * (days + k), transcendentals=0
        ),
        compiler_params=pltpu.CompilerParams(vmem_limit_bytes=WIDE_LIMIT),
    )(core, pcs, field)


def first_kernel(recv_ref, sent_ref, loadings_ref, padded_ref):
    loadings = recv_ref[0] + recv_ref[1] + recv_ref[2] + recv_ref[3]
    k = loadings.shape[0]
    padded_ref[...] = jnp.zeros_like(padded_ref)
    padded_ref[0:k] = loadings
    loadings_ref[...] = loadings
    loadings = padded_ref[...]
    sent_ref[0:PAD] = rows_nt(loadings * loadings * loadings, loadings)
    sent_ref[PAD : 2 * PAD] = rows_nt(loadings, loadings)


def first(recv):
    k, share = recv.shape[1:]
    return pl.pallas_call(
        first_kernel,
        out_shape=(
            jax.ShapeDtypeStruct((2 * PAD, PAD), F32),
            jax.ShapeDtypeStruct((k, share), F32),
            jax.ShapeDtypeStruct((PAD, share), F32),
        ),
        in_specs=[VMEM],
        out_specs=(VMEM, VMEM, VMEM),
        compiler_params=pltpu.CompilerParams(vmem_limit_bytes=LIMIT),
    )(recv)


def second_kernel(cells, got_ref, loadings_ref, sent_ref, y_ref):
    corr = got_ref[PAD : 2 * PAD]
    rows = lax.broadcasted_iota(jnp.int32, corr.shape, 0)
    columns = lax.broadcasted_iota(jnp.int32, corr.shape, 1)
    colsq = jnp.sum(jnp.where(rows == columns, corr, 0.0), axis=1, keepdims=True)
    y = polar_rows(got_ref[0:PAD] - corr * colsq * (1.0 / cells))
    y_ref[...] = y
    sent_ref[...] = turn_cube(y, loadings_ref[...])


def next_y(cells, cube_ref, got_ref, y_ref):
    y = y_ref[...]
    cross = small_nn(y, got_ref[PAD : 2 * PAD])
    colsq = jnp.sum(y * cross, axis=1, keepdims=True)
    return polar_rows(cube_ref[...] - cross * colsq * (1.0 / cells))


def third_kernel(cells, cube_ref, got_ref, y_ref, loadings_ref, sent_ref, out_ref):
    y = next_y(cells, cube_ref, got_ref, y_ref)
    out_ref[...] = y
    sent_ref[...] = turn_cube(y, loadings_ref[...])


def last_kernel(cells, cube_ref, got_ref, y_ref, loadings_ref, terms_ref, rotated_ref, series_ref):
    k = rotated_ref.shape[0]
    y = next_y(cells, cube_ref, got_ref, y_ref)
    rotated_ref[...] = small_nn(y, loadings_ref[...])[0:k]
    series_ref[...] = rows_nt(y, terms_ref[...])[0:k]


def whole(kernel, outs, *args):
    return pl.pallas_call(
        kernel,
        out_shape=tuple(jax.ShapeDtypeStruct(s, F32) for s in outs),
        in_specs=[VMEM] * len(args),
        out_specs=(VMEM,) * len(outs),
        compiler_params=pltpu.CompilerParams(vmem_limit_bytes=LIMIT),
    )(*args)


def terms_kernel(scale, where_ref, field_ref, near_ref, far_ref, out_ref):
    row, core = where_ref[0], where_ref[1]
    share = near_ref.shape[2]
    total = jnp.zeros(out_ref.shape, F32)
    for d in range(Y):
        group = CORE * lax.rem(row + Y - d, Y)
        for owner, loadings in ((core, near_ref[d]), (1 - core, far_ref[d])):
            lh, ll = split(pad_rows(loadings, PAD))
            high, low = split(columns(field_ref, group + owner, share))
            total += fold(nt(high, jnp.concatenate([lh, ll], axis=0))) + nt(low, lh)
    out_ref[...] = total * scale


def series_terms(field, near, far, where, scale):
    days = field.shape[0]
    rows, share = near.shape[1:]
    return pl.pallas_call(
        functools.partial(terms_kernel, scale),
        out_shape=jax.ShapeDtypeStruct((days, PAD), F32),
        in_specs=[pl.BlockSpec(memory_space=pltpu.SMEM), VMEM, VMEM, VMEM],
        out_specs=VMEM,
        cost_estimate=pl.CostEstimate(
            flops=6 * days * PAD * share * Y * CORE,
            bytes_accessed=4 * Y * CORE * share * (days + rows),
            transcendentals=0,
        ),
        compiler_params=pltpu.CompilerParams(vmem_limit_bytes=LIMIT),
    )(where, field, near, far)


def swap(value, axes):
    return lax.all_to_all(value, axes, 0, 0)


def spread(value, count):
    return jnp.broadcast_to(value, (count,) + value.shape)


def on_device(field, pcs):
    k, days_here = pcs.shape
    groups = Y * CORE
    days_total = days_here * groups
    cells_total = field.shape[1] * Z * X
    share = field.shape[1] // groups
    core = lax.axis_index("core").astype(jnp.int32)
    row = lax.axis_index("y").astype(jnp.int32)

    scale = 1.0 / days_total**0.5
    theirs = lax.ppermute(parts(field, pcs, (1 - core)[None], scale), "core", [(0, 1), (1, 0)])
    recv = swap(theirs + parts(field, pcs, core[None], scale), "y")
    sent, narrow, loadings = first(recv)

    chunk = swap(sent.reshape(N_PLANE, 2 * ROWS, PAD), PLANE)
    near = [lax.ppermute(narrow, "y", [(i, (i + d) % Y) for i in range(Y)]) for d in range(1, Y)]
    chunk = swap(spread(jnp.sum(chunk, axis=0), Z), "z")
    base = swap(spread(jnp.sum(chunk, axis=0), N_PLANE), PLANE)
    base, near = lax.optimization_barrier((base, near))
    near = jnp.stack([narrow] + near)
    far = lax.ppermute(near, "core", [(0, 1), (1, 0)])
    base = base.reshape(2 * PAD, PAD)
    piece = days_here // Z
    sent, y = whole(functools.partial(second_kernel, cells_total), [(PAD, PAD)] * 2, base, loadings)

    sent, near, far = lax.optimization_barrier((sent, near, far))
    terms = series_terms(field, near, far, jnp.stack([row, core]), days_total**0.5 / cells_total)
    chunk, terms = lax.optimization_barrier((swap(sent.reshape(N_PLANE, ROWS, PAD), PLANE), terms))
    chunk = jnp.sum(chunk, axis=0)
    both = jnp.concatenate([spread(chunk, Z), terms.reshape(Z, piece, PAD)], axis=1)
    both = jnp.sum(swap(both, "z"), axis=0)
    got = swap(spread(both, N_PLANE), PLANE)
    cube = got[:, :ROWS].reshape(PAD, PAD)
    terms = got[:, ROWS:].reshape(X, groups, piece, PAD)
    terms = jnp.sum(lax.dynamic_index_in_dim(terms, row * CORE + core, 1, keepdims=False), axis=0)
    sent, y = whole(
        functools.partial(third_kernel, cells_total), [(PAD, PAD)] * 2, cube, base, y, loadings
    )

    chunk = jnp.sum(swap(sent.reshape(N_PLANE, ROWS, PAD), PLANE), axis=0)
    got = swap(spread(jnp.concatenate([chunk, terms], axis=0), Z), "z")
    terms = got[:, ROWS:].reshape(days_here, PAD)
    chunk, terms = lax.optimization_barrier((jnp.sum(got[:, :ROWS], axis=0), terms))
    cube = swap(spread(chunk, N_PLANE), PLANE).reshape(PAD, PAD)
    return whole(
        functools.partial(last_kernel, cells_total),
        [(k, share), (k, days_here)],
        cube, base, y, loadings, terms,
    )


def solution(mesh):
    split_mesh = Mesh(mesh.devices.reshape(Z, X, Y, CORE), ("z", "x", "y", "core"))
    placed = (P(DAY, ("z", "x")), P(None, DAY))
    return jax.shard_map(
        on_device,
        mesh=split_mesh,
        in_specs=placed,
        out_specs=(P(None, ("z", "x", "y", "core")), P(None, DAY)),
        check_vma=False,
    )
```

```python
import functools

import jax
import jax.numpy as jnp
from jax import lax
from jax.experimental import pallas as pl
from jax.experimental.pallas import tpu as pltpu
from jax.sharding import Mesh, PartitionSpec as P

ITERS = 3
NS_STEPS = 12
Z, X, Y, CORE = 16, 4, 4, 2
PLANE = ("x", "y", "core")
DAY = ("y", "core")
PAD = 128
N_PLANE = X * Y * CORE
ROWS = PAD // N_PLANE
F32 = jnp.float32
VMEM = pl.BlockSpec(memory_space=pltpu.VMEM)
LIMIT = 24 << 20
FLOPS = 5000000000
WIDE_LIMIT = 52 << 20


def split(value):
    high = value.astype(jnp.bfloat16)
    return high, (value - high.astype(F32)).astype(jnp.bfloat16)


def nn(left, right):
    return jnp.dot(left, right, preferred_element_type=F32)


def nt(left, right):
    return lax.dot_general(left, right, (((1,), (1,)), ((), ())), preferred_element_type=F32)


def fold(value):
    half = value.shape[1] // 2
    return value[:, :half] + value[:, half:]


def pad_rows(value, rows):
    return jnp.concatenate([value, jnp.zeros((rows - value.shape[0], value.shape[1]), F32)], axis=0)


def small_nn(left, right):
    lh, ll = split(left)
    rh, rl = split(right)
    both = jnp.concatenate([rh, rl], axis=1)
    return fold(nn(jnp.concatenate([lh, ll], axis=1), jnp.concatenate([both, both], axis=0)))


def rows_nt(left, right):
    lh, ll = split(left)
    rh, rl = split(right)
    return fold(nt(lh, jnp.concatenate([rh, rl], axis=0))) + nt(ll, rh)


def polar_rows(grad):
    norm = jnp.sqrt(jnp.sum(jnp.sum(grad * grad, axis=1, keepdims=True), axis=0, keepdims=True))
    y = grad / (norm + 1e-06)
    for step in range(NS_STEPS):
        high, low = split(y)
        down = jnp.concatenate([high, low], axis=0)
        across = jnp.concatenate([high, low], axis=1)
        inner = fold(nt(across, jnp.concatenate([down, down], axis=1)))
        ih, il = split(inner)
        again = jnp.concatenate([across, across], axis=0)
        y = 1.5 * y - 0.5 * fold(nn(jnp.concatenate([ih, il], axis=1), again))
    return y


def turn_cube(y, loadings):
    turned = small_nn(y, loadings)
    return rows_nt(turned * turned * turned, loadings)


def columns(field_ref, group, share):
    return field_ref[:, pl.ds(pl.multiple_of(group * share, share), share)]


def parts_kernel(scale, core_ref, pcs_ref, field_ref, out_ref, pcs, wide, field, sems):
    share = out_ref.shape[2]
    copies = [pltpu.make_async_copy(pcs_ref, pcs, sems.at[Y])]
    for g in range(Y):
        start = pl.multiple_of((CORE * g + core_ref[0]) * share, share)
        copies.append(pltpu.make_async_copy(field_ref.at[:, pl.ds(start, share)], field.at[g], sems.at[g]))
    for copy in copies:
        copy.start()
    wide[...] = jnp.zeros_like(wide)
    copies[0].wait()
    wide[0 : pcs.shape[0]] = pcs[...] * scale
    half = wide.shape[0]
    left_high, left_low = split(wide[...])
    left = jnp.concatenate([left_high, left_low], axis=0)
    for g in range(Y):
        copies[1 + g].wait()
        high, low = split(field[g])
        both = nn(left, high)
        total = both[0:half] + both[half : 2 * half] + nn(left_high, low)
        out_ref[g] = total[0 : out_ref.shape[1]]


def parts(field, pcs, core, scale):
    k, days = pcs.shape
    share = field.shape[1] // (Y * CORE)
    half = (k + 15) // 16 * 16
    rows = (k + 7) // 8 * 8
    far = pl.BlockSpec(memory_space=pl.ANY)
    return pl.pallas_call(
        functools.partial(parts_kernel, scale),
        out_shape=jax.ShapeDtypeStruct((Y, rows, share), F32),
        in_specs=[pl.BlockSpec(memory_space=pltpu.SMEM), far, far],
        out_specs=VMEM,
        scratch_shapes=[
            pltpu.VMEM((k, days), F32),
            pltpu.VMEM((half, days), F32),
            pltpu.VMEM((Y, days, share), F32),
            pltpu.SemaphoreType.DMA((Y + 1,)),
        ],
        cost_estimate=pl.CostEstimate(
            flops=6 * k * days * share * Y, bytes_accessed=4 * Y * share * (days + k), transcendentals=0
        ),
        compiler_params=pltpu.CompilerParams(vmem_limit_bytes=WIDE_LIMIT),
    )(core, pcs, field)


def first_kernel(recv_ref, sent_ref, loadings_ref, padded_ref):
    loadings = recv_ref[0] + recv_ref[1] + recv_ref[2] + recv_ref[3]
    k = loadings.shape[0]
    padded_ref[...] = jnp.zeros_like(padded_ref)
    padded_ref[0:k] = loadings
    loadings_ref[...] = loadings
    loadings = padded_ref[...]
    sent_ref[0:PAD] = rows_nt(loadings * loadings * loadings, loadings)
    sent_ref[PAD : 2 * PAD] = rows_nt(loadings, loadings)


def first(recv):
    k, share = recv.shape[1:]
    return pl.pallas_call(
        first_kernel,
        out_shape=(
            jax.ShapeDtypeStruct((2 * PAD, PAD), F32),
            jax.ShapeDtypeStruct((k, share), F32),
            jax.ShapeDtypeStruct((PAD, share), F32),
        ),
        in_specs=[VMEM],
        out_specs=(VMEM, VMEM, VMEM),
        compiler_params=pltpu.CompilerParams(vmem_limit_bytes=LIMIT),
    )(recv)


def second_kernel(cells, got_ref, loadings_ref, sent_ref, y_ref):
    corr = got_ref[PAD : 2 * PAD]
    rows = lax.broadcasted_iota(jnp.int32, corr.shape, 0)
    columns = lax.broadcasted_iota(jnp.int32, corr.shape, 1)
    colsq = jnp.sum(jnp.where(rows == columns, corr, 0.0), axis=1, keepdims=True)
    y = polar_rows(got_ref[0:PAD] - corr * colsq * (1.0 / cells))
    y_ref[...] = y
    sent_ref[...] = turn_cube(y, loadings_ref[...])


def next_y(cells, cube_ref, got_ref, y_ref):
    y = y_ref[...]
    cross = small_nn(y, got_ref[PAD : 2 * PAD])
    colsq = jnp.sum(y * cross, axis=1, keepdims=True)
    return polar_rows(cube_ref[...] - cross * colsq * (1.0 / cells))


def third_kernel(cells, cube_ref, got_ref, y_ref, loadings_ref, sent_ref, out_ref):
    y = next_y(cells, cube_ref, got_ref, y_ref)
    out_ref[...] = y
    sent_ref[...] = turn_cube(y, loadings_ref[...])


def last_kernel(cells, cube_ref, got_ref, y_ref, loadings_ref, terms_ref, rotated_ref, series_ref):
    k = rotated_ref.shape[0]
    y = next_y(cells, cube_ref, got_ref, y_ref)
    rotated_ref[...] = small_nn(y, loadings_ref[...])[0:k]
    series_ref[...] = rows_nt(y, terms_ref[...])[0:k]


def whole(kernel, outs, *args):
    return pl.pallas_call(
        kernel,
        out_shape=tuple(jax.ShapeDtypeStruct(s, F32) for s in outs),
        in_specs=[VMEM] * len(args),
        out_specs=(VMEM,) * len(outs),
        cost_estimate=pl.CostEstimate(flops=FLOPS, bytes_accessed=0, transcendentals=0),
        compiler_params=pltpu.CompilerParams(vmem_limit_bytes=LIMIT),
    )(*args)


def terms_kernel(scale, where_ref, field_ref, near_ref, far_ref, out_ref):
    row, core = where_ref[0], where_ref[1]
    share = near_ref.shape[2]
    total = jnp.zeros(out_ref.shape, F32)
    for d in range(Y):
        group = CORE * lax.rem(row + Y - d, Y)
        for owner, loadings in ((core, near_ref[d]), (1 - core, far_ref[d])):
            lh, ll = split(pad_rows(loadings, PAD))
            high, low = split(columns(field_ref, group + owner, share))
            total += fold(nt(high, jnp.concatenate([lh, ll], axis=0))) + nt(low, lh)
    out_ref[...] = total * scale


def series_terms(field, near, far, where, scale):
    days = field.shape[0]
    rows, share = near.shape[1:]
    return pl.pallas_call(
        functools.partial(terms_kernel, scale),
        out_shape=jax.ShapeDtypeStruct((days, PAD), F32),
        in_specs=[pl.BlockSpec(memory_space=pltpu.SMEM), VMEM, VMEM, VMEM],
        out_specs=VMEM,
        cost_estimate=pl.CostEstimate(
            flops=6 * days * PAD * share * Y * CORE,
            bytes_accessed=4 * Y * CORE * share * (days + rows),
            transcendentals=0,
        ),
        compiler_params=pltpu.CompilerParams(vmem_limit_bytes=LIMIT),
    )(where, field, near, far)


def swap(value, axes):
    return lax.all_to_all(value, axes, 0, 0)


def spread(value, count):
    return jnp.broadcast_to(value, (count,) + value.shape)


def on_device(field, pcs):
    k, days_here = pcs.shape
    groups = Y * CORE
    days_total = days_here * groups
    cells_total = field.shape[1] * Z * X
    share = field.shape[1] // groups
    core = lax.axis_index("core").astype(jnp.int32)
    row = lax.axis_index("y").astype(jnp.int32)

    scale = 1.0 / days_total**0.5
    theirs = lax.ppermute(parts(field, pcs, (1 - core)[None], scale), "core", [(0, 1), (1, 0)])
    recv = swap(theirs + parts(field, pcs, core[None], scale), "y")
    sent, narrow, loadings = first(recv)

    chunk = swap(sent.reshape(N_PLANE, 2 * ROWS, PAD), PLANE)
    near = [lax.ppermute(narrow, "y", [(i, (i + d) % Y) for i in range(Y)]) for d in range(1, Y)]
    chunk = swap(spread(jnp.sum(chunk, axis=0), Z), "z")
    base = swap(spread(jnp.sum(chunk, axis=0), N_PLANE), PLANE)
    base = base.reshape(2 * PAD, PAD)
    piece = days_here // Z
    sent, y = whole(functools.partial(second_kernel, cells_total), [(PAD, PAD)] * 2, base, loadings)

    sent, near = lax.optimization_barrier((sent, near))
    near = jnp.stack([narrow] + near)
    far = lax.ppermute(near, "core", [(0, 1), (1, 0)])
    terms = series_terms(field, near, far, jnp.stack([row, core]), days_total**0.5 / cells_total)
    chunk, terms = lax.optimization_barrier((swap(sent.reshape(N_PLANE, ROWS, PAD), PLANE), terms))
    chunk = jnp.sum(chunk, axis=0)
    both = jnp.concatenate([spread(chunk, Z), terms.reshape(Z, piece, PAD)], axis=1)
    both = jnp.sum(swap(both, "z"), axis=0)
    got = swap(spread(both, N_PLANE), PLANE)
    cube = got[:, :ROWS].reshape(PAD, PAD)
    terms = got[:, ROWS:].reshape(X, groups, piece, PAD)
    terms = jnp.sum(lax.dynamic_index_in_dim(terms, row * CORE + core, 1, keepdims=False), axis=0)
    sent, y = whole(
        functools.partial(third_kernel, cells_total), [(PAD, PAD)] * 2, cube, base, y, loadings
    )

    chunk = jnp.sum(swap(sent.reshape(N_PLANE, ROWS, PAD), PLANE), axis=0)
    got = swap(spread(jnp.concatenate([chunk, terms], axis=0), Z), "z")
    terms = got[:, ROWS:].reshape(days_here, PAD)
    chunk, terms = lax.optimization_barrier((jnp.sum(got[:, :ROWS], axis=0), terms))
    cube = swap(spread(chunk, N_PLANE), PLANE).reshape(PAD, PAD)
    return whole(
        functools.partial(last_kernel, cells_total),
        [(k, share), (k, days_here)],
        cube, base, y, loadings, terms,
    )


def solution(mesh):
    split_mesh = Mesh(mesh.devices.reshape(Z, X, Y, CORE), ("z", "x", "y", "core"))
    placed = (P(DAY, ("z", "x")), P(None, DAY))
    return jax.shard_map(
        on_device,
        mesh=split_mesh,
        in_specs=placed,
        out_specs=(P(None, ("z", "x", "y", "core")), P(None, DAY)),
        check_vma=False,
    )
```

```python
import functools

import jax
import jax.numpy as jnp
from jax import lax
from jax.experimental import pallas as pl
from jax.experimental.pallas import tpu as pltpu
from jax.sharding import Mesh, PartitionSpec as P

ITERS = 3
NS_STEPS = 12
Z, X, Y, CORE = 16, 4, 4, 2
PLANE = ("x", "y", "core")
DAY = ("y", "core")
PAD = 128
N_PLANE = X * Y * CORE
ROWS = PAD // N_PLANE
F32 = jnp.float32
VMEM = pl.BlockSpec(memory_space=pltpu.VMEM)
LIMIT = 24 << 20
FLOPS = 5000000000
WIDE_LIMIT = 48 << 20
TERMS_LIMIT = 51 << 20


def split(value):
    high = value.astype(jnp.bfloat16)
    return high, (value - high.astype(F32)).astype(jnp.bfloat16)


def nn(left, right):
    return jnp.dot(left, right, preferred_element_type=F32)


def nt(left, right):
    return lax.dot_general(left, right, (((1,), (1,)), ((), ())), preferred_element_type=F32)


def fold(value):
    half = value.shape[1] // 2
    return value[:, :half] + value[:, half:]


def pad_rows(value, rows):
    return jnp.concatenate([value, jnp.zeros((rows - value.shape[0], value.shape[1]), F32)], axis=0)


def small_nn(left, right):
    lh, ll = split(left)
    rh, rl = split(right)
    both = jnp.concatenate([rh, rl], axis=1)
    return fold(nn(jnp.concatenate([lh, ll], axis=1), jnp.concatenate([both, both], axis=0)))


def rows_nt(left, right):
    lh, ll = split(left)
    rh, rl = split(right)
    return fold(nt(lh, jnp.concatenate([rh, rl], axis=0))) + nt(ll, rh)


def polar_rows(grad):
    norm = jnp.sqrt(jnp.sum(jnp.sum(grad * grad, axis=1, keepdims=True), axis=0, keepdims=True))
    y = grad / (norm + 1e-06)
    for step in range(NS_STEPS):
        high, low = split(y)
        inner = fold(nt(high, jnp.concatenate([high, low], axis=0))) + nt(low, high)
        ih, il = split(inner)
        y = 1.5 * y - 0.5 * (fold(nn(ih, jnp.concatenate([high, low], axis=1))) + nn(il, high))
    return y


def turn_cube(y, loadings):
    turned = small_nn(y, loadings)
    return rows_nt(turned * turned * turned, loadings)


def columns(field_ref, group, share):
    return field_ref[:, pl.ds(pl.multiple_of(group * share, share), share)]


def some_parts(left_high, left_low, field_ref, out_ref, owner, ready):
    left = jnp.concatenate([left_high, left_low], axis=0)
    half = left_high.shape[0]
    for g in range(Y):
        ready(g)
        high, low = split(columns(field_ref, CORE * g + owner, out_ref.shape[2]))
        both = nn(left, high)
        total = both[0:half] + both[half : 2 * half] + nn(left_high, low)
        out_ref[g] = total[0 : out_ref.shape[1]]


def scaled(pcs, wide, scale):
    wide[...] = jnp.zeros_like(wide)
    wide[0 : pcs.shape[0]] = pcs * scale
    return split(wide[...])


def their_parts_kernel(scale, core_ref, pcs_ref, field_ref, out_ref, kept_ref, wide, sems):
    share = out_ref.shape[2]
    theirs = 1 - core_ref[0]
    copies = []
    for owner in (theirs, core_ref[0]):
        for g in range(Y):
            place = pl.ds(pl.multiple_of((CORE * g + owner) * share, share), share)
            copies.append(
                pltpu.make_async_copy(field_ref.at[:, place], kept_ref.at[:, place], sems.at[len(copies)])
            )
    for copy in copies:
        copy.start()
    left_high, left_low = scaled(pcs_ref[...], wide, scale)
    some_parts(left_high, left_low, kept_ref, out_ref, theirs, lambda g: copies[g].wait())
    for copy in copies[Y:]:
        copy.wait()


def own_parts_kernel(scale, core_ref, pcs_ref, kept_ref, out_ref, wide):
    left_high, left_low = scaled(pcs_ref[...], wide, scale)
    some_parts(left_high, left_low, kept_ref, out_ref, core_ref[0], lambda g: None)


def their_parts(field, pcs, core, scale):
    k, days = pcs.shape
    share = field.shape[1] // (Y * CORE)
    half = (k + 15) // 16 * 16
    rows = (k + 7) // 8 * 8
    return pl.pallas_call(
        functools.partial(their_parts_kernel, scale),
        out_shape=(jax.ShapeDtypeStruct((Y, rows, share), F32), jax.ShapeDtypeStruct(field.shape, F32)),
        in_specs=[pl.BlockSpec(memory_space=pltpu.SMEM), VMEM, pl.BlockSpec(memory_space=pl.ANY)],
        out_specs=(VMEM, VMEM),
        scratch_shapes=[pltpu.VMEM((half, days), F32), pltpu.SemaphoreType.DMA((Y * CORE,))],
        cost_estimate=pl.CostEstimate(
            flops=6 * k * days * share * Y, bytes_accessed=4 * days * (field.shape[1] + k), transcendentals=0
        ),
        compiler_params=pltpu.CompilerParams(vmem_limit_bytes=WIDE_LIMIT),
    )(core, pcs, field)


def own_parts(kept, pcs, core, scale):
    k, days = pcs.shape
    share = kept.shape[1] // (Y * CORE)
    half = (k + 15) // 16 * 16
    rows = (k + 7) // 8 * 8
    return pl.pallas_call(
        functools.partial(own_parts_kernel, scale),
        out_shape=jax.ShapeDtypeStruct((Y, rows, share), F32),
        in_specs=[pl.BlockSpec(memory_space=pltpu.SMEM), VMEM, VMEM],
        out_specs=VMEM,
        scratch_shapes=[pltpu.VMEM((half, days), F32)],
        cost_estimate=pl.CostEstimate(flops=6 * k * days * share * Y, bytes_accessed=0, transcendentals=0),
        compiler_params=pltpu.CompilerParams(vmem_limit_bytes=LIMIT),
    )(core, pcs, kept)


def first_kernel(recv_ref, sent_ref, loadings_ref, padded_ref):
    loadings = recv_ref[0] + recv_ref[1] + recv_ref[2] + recv_ref[3]
    k = loadings.shape[0]
    padded_ref[...] = jnp.zeros_like(padded_ref)
    padded_ref[0:k] = loadings
    loadings_ref[...] = loadings
    loadings = padded_ref[...]
    sent_ref[0:PAD] = rows_nt(loadings * loadings * loadings, loadings)
    sent_ref[PAD : 2 * PAD] = rows_nt(loadings, loadings)


def first(recv):
    k, share = recv.shape[1:]
    return pl.pallas_call(
        first_kernel,
        out_shape=(
            jax.ShapeDtypeStruct((2 * PAD, PAD), F32),
            jax.ShapeDtypeStruct((k, share), F32),
            jax.ShapeDtypeStruct((PAD, share), F32),
        ),
        in_specs=[VMEM],
        out_specs=(VMEM, VMEM, VMEM),
        compiler_params=pltpu.CompilerParams(vmem_limit_bytes=LIMIT),
    )(recv)


def second_kernel(cells, got_ref, loadings_ref, sent_ref, y_ref):
    corr = got_ref[PAD : 2 * PAD]
    rows = lax.broadcasted_iota(jnp.int32, corr.shape, 0)
    columns = lax.broadcasted_iota(jnp.int32, corr.shape, 1)
    colsq = jnp.sum(jnp.where(rows == columns, corr, 0.0), axis=1, keepdims=True)
    y = polar_rows(got_ref[0:PAD] - corr * colsq * (1.0 / cells))
    y_ref[...] = y
    sent_ref[...] = turn_cube(y, loadings_ref[...])


def next_y(cells, cube_ref, got_ref, y_ref):
    y = y_ref[...]
    cross = small_nn(y, got_ref[PAD : 2 * PAD])
    colsq = jnp.sum(y * cross, axis=1, keepdims=True)
    return polar_rows(cube_ref[...] - cross * colsq * (1.0 / cells))


def third_kernel(cells, cube_ref, got_ref, y_ref, loadings_ref, sent_ref, out_ref):
    y = next_y(cells, cube_ref, got_ref, y_ref)
    out_ref[...] = y
    sent_ref[...] = turn_cube(y, loadings_ref[...])


def last_kernel(cells, cube_ref, got_ref, y_ref, loadings_ref, terms_ref, rotated_ref, series_ref):
    k = rotated_ref.shape[0]
    y = next_y(cells, cube_ref, got_ref, y_ref)
    rotated_ref[...] = small_nn(y, loadings_ref[...])[0:k]
    series_ref[...] = rows_nt(y, terms_ref[...])[0:k]


def whole(kernel, outs, *args):
    return pl.pallas_call(
        kernel,
        out_shape=tuple(jax.ShapeDtypeStruct(s, F32) for s in outs),
        in_specs=[VMEM] * len(args),
        out_specs=(VMEM,) * len(outs),
        cost_estimate=pl.CostEstimate(flops=FLOPS, bytes_accessed=0, transcendentals=0),
        compiler_params=pltpu.CompilerParams(vmem_limit_bytes=LIMIT),
    )(*args)


def terms_kernel(scale, where_ref, field_ref, near_ref, far_ref, out_ref, field, sems):
    row, core = where_ref[0], where_ref[1]
    share = near_ref.shape[2]
    copies = []
    for d in range(Y):
        for owner in (core, 1 - core):
            start = pl.multiple_of((CORE * (row ^ d) + owner) * share, share)
            slot = len(copies)
            copies.append(
                pltpu.make_async_copy(field_ref.at[:, pl.ds(start, share)], field.at[slot], sems.at[slot])
            )
    for copy in copies:
        copy.start()
    total = jnp.zeros(out_ref.shape, F32)
    for slot in range(Y * CORE):
        lh, ll = split(pad_rows((far_ref if slot % CORE else near_ref)[slot // CORE], PAD))
        copies[slot].wait()
        high, low = split(field[slot])
        total += fold(nt(high, jnp.concatenate([lh, ll], axis=0))) + nt(low, lh)
    out_ref[...] = total * scale


def series_terms(field, near, far, where, scale):
    days = field.shape[0]
    rows, share = near.shape[1:]
    return pl.pallas_call(
        functools.partial(terms_kernel, scale),
        out_shape=jax.ShapeDtypeStruct((days, PAD), F32),
        in_specs=[
            pl.BlockSpec(memory_space=pltpu.SMEM),
            pl.BlockSpec(memory_space=pl.ANY),
            VMEM,
            VMEM,
        ],
        out_specs=VMEM,
        scratch_shapes=[pltpu.VMEM((Y * CORE, days, share), F32), pltpu.SemaphoreType.DMA((Y * CORE,))],
        cost_estimate=pl.CostEstimate(
            flops=6 * days * PAD * share * Y * CORE,
            bytes_accessed=4 * Y * CORE * share * (days + rows),
            transcendentals=0,
        ),
        compiler_params=pltpu.CompilerParams(vmem_limit_bytes=TERMS_LIMIT),
    )(where, field, near, far)


def swap(value, axes):
    return lax.all_to_all(value, axes, 0, 0)


def spread(value, count):
    return jnp.broadcast_to(value, (count,) + value.shape)


def on_device(field, pcs):
    k, days_here = pcs.shape
    groups = Y * CORE
    days_total = days_here * groups
    cells_total = field.shape[1] * Z * X
    share = field.shape[1] // groups
    core = lax.axis_index("core").astype(jnp.int32)
    row = lax.axis_index("y").astype(jnp.int32)

    scale = 1.0 / days_total**0.5
    theirs, kept = their_parts(field, pcs, core[None], scale)
    theirs = lax.ppermute(theirs, "core", [(0, 1), (1, 0)])
    recv = swap(theirs + own_parts(kept, pcs, core[None], scale), "y")
    sent, narrow, loadings = first(recv)

    chunk = swap(sent.reshape(N_PLANE, 2 * ROWS, PAD), PLANE)
    near = lax.ppermute(narrow, "y", [(i, i ^ 1) for i in range(Y)])
    chunk = swap(spread(jnp.sum(chunk, axis=0), Z), "z")
    chunk, near = lax.optimization_barrier((chunk, near))
    pair = jnp.stack([narrow, near])
    near = lax.ppermute(pair, "y", [(i, i ^ 2) for i in range(Y)])
    base = swap(spread(jnp.sum(chunk, axis=0), N_PLANE), PLANE)
    base = base.reshape(2 * PAD, PAD)
    piece = days_here // Z
    sent, y = whole(functools.partial(second_kernel, cells_total), [(PAD, PAD)] * 2, base, loadings)

    sent, near = lax.optimization_barrier((sent, near))
    near = jnp.concatenate([pair, near], axis=0)
    far = lax.ppermute(near, "core", [(0, 1), (1, 0)])
    terms = series_terms(field, near, far, jnp.stack([row, core]), days_total**0.5 / cells_total)
    chunk, terms = lax.optimization_barrier((swap(sent.reshape(N_PLANE, ROWS, PAD), PLANE), terms))
    chunk = jnp.sum(chunk, axis=0)
    both = jnp.concatenate([spread(chunk, Z), terms.reshape(Z, piece, PAD)], axis=1)
    both = jnp.sum(swap(both, "z"), axis=0)
    got = swap(spread(both, N_PLANE), PLANE)
    cube = got[:, :ROWS].reshape(PAD, PAD)
    terms = got[:, ROWS:].reshape(X, groups, piece, PAD)
    terms = jnp.sum(lax.dynamic_index_in_dim(terms, row * CORE + core, 1, keepdims=False), axis=0)
    sent, y = whole(
        functools.partial(third_kernel, cells_total), [(PAD, PAD)] * 2, cube, base, y, loadings
    )

    chunk = jnp.sum(swap(sent.reshape(N_PLANE, ROWS, PAD), PLANE), axis=0)
    got = swap(spread(jnp.concatenate([chunk, terms], axis=0), Z), "z")
    terms = got[:, ROWS:].reshape(days_here, PAD)
    chunk, terms = lax.optimization_barrier((jnp.sum(got[:, :ROWS], axis=0), terms))
    cube = swap(spread(chunk, N_PLANE), PLANE).reshape(PAD, PAD)
    return whole(
        functools.partial(last_kernel, cells_total),
        [(k, share), (k, days_here)],
        cube, base, y, loadings, terms,
    )


def solution(mesh):
    split_mesh = Mesh(mesh.devices.reshape(Z, X, Y, CORE), ("z", "x", "y", "core"))
    placed = (P(DAY, ("z", "x")), P(None, DAY))
    return jax.shard_map(
        on_device,
        mesh=split_mesh,
        in_specs=placed,
        out_specs=(P(None, ("z", "x", "y", "core")), P(None, DAY)),
        check_vma=False,
    )
```

```python
import functools

import jax
import jax.numpy as jnp
from jax import lax
from jax.experimental import pallas as pl
from jax.experimental.pallas import tpu as pltpu
from jax.sharding import Mesh, PartitionSpec as P

ITERS = 3
NS_STEPS = 12
Z, X, Y, CORE = 16, 4, 4, 2
PLANE = ("x", "y", "core")
DAY = ("y", "core")
PAD = 128
N_PLANE = X * Y * CORE
ROWS = PAD // N_PLANE
F32 = jnp.float32
VMEM = pl.BlockSpec(memory_space=pltpu.VMEM)
LIMIT = 24 << 20
WIDE_LIMIT = 52 << 20


def split(value):
    high = value.astype(jnp.bfloat16)
    return high, (value - high.astype(F32)).astype(jnp.bfloat16)


def nn(left, right):
    return jnp.dot(left, right, preferred_element_type=F32)


def nt(left, right):
    return lax.dot_general(left, right, (((1,), (1,)), ((), ())), preferred_element_type=F32)


def fold(value):
    half = value.shape[1] // 2
    return value[:, :half] + value[:, half:]


def pad_rows(value, rows):
    return jnp.concatenate([value, jnp.zeros((rows - value.shape[0], value.shape[1]), F32)], axis=0)


def small_nn(left, right):
    lh, ll = split(left)
    rh, rl = split(right)
    both = jnp.concatenate([rh, rl], axis=1)
    return fold(nn(jnp.concatenate([lh, ll], axis=1), jnp.concatenate([both, both], axis=0)))


def rows_nt(left, right):
    lh, ll = split(left)
    rh, rl = split(right)
    return fold(nt(lh, jnp.concatenate([rh, rl], axis=0))) + nt(ll, rh)


def polar_rows(grad):
    norm = jnp.sqrt(jnp.sum(jnp.sum(grad * grad, axis=1, keepdims=True), axis=0, keepdims=True))
    y = grad / (norm + 1e-06)
    for step in range(NS_STEPS):
        high, low = split(y)
        inner = fold(nt(high, jnp.concatenate([high, low], axis=0))) + nt(low, high)
        ih, il = split(inner)
        y = 1.5 * y - 0.5 * (fold(nn(ih, jnp.concatenate([high, low], axis=1))) + nn(il, high))
    return y


def turn_cube(y, loadings):
    turned = small_nn(y, loadings)
    return rows_nt(turned * turned * turned, loadings)


def columns(field_ref, group, share):
    return field_ref[:, pl.ds(pl.multiple_of(group * share, share), share)]


def parts_kernel(scale, core_ref, pcs_ref, field_ref, out_ref, pcs, wide, field, sems):
    share = out_ref.shape[2]
    copies = [pltpu.make_async_copy(pcs_ref, pcs, sems.at[Y])]
    for g in range(Y):
        start = pl.multiple_of((CORE * g + core_ref[0]) * share, share)
        copies.append(pltpu.make_async_copy(field_ref.at[:, pl.ds(start, share)], field.at[g], sems.at[g]))
    for copy in copies:
        copy.start()
    wide[...] = jnp.zeros_like(wide)
    copies[0].wait()
    wide[0 : pcs.shape[0]] = pcs[...] * scale
    half = wide.shape[0]
    left_high, left_low = split(wide[...])
    left = jnp.concatenate([left_high, left_low], axis=0)
    for g in range(Y):
        copies[1 + g].wait()
        high, low = split(field[g])
        both = nn(left, high)
        total = both[0:half] + both[half : 2 * half] + nn(left_high, low)
        out_ref[g] = total[0 : out_ref.shape[1]]


def parts(field, pcs, core, scale):
    k, days = pcs.shape
    share = field.shape[1] // (Y * CORE)
    half = (k + 15) // 16 * 16
    rows = (k + 7) // 8 * 8
    far = pl.BlockSpec(memory_space=pl.ANY)
    return pl.pallas_call(
        functools.partial(parts_kernel, scale),
        out_shape=jax.ShapeDtypeStruct((Y, rows, share), F32),
        in_specs=[pl.BlockSpec(memory_space=pltpu.SMEM), far, far],
        out_specs=VMEM,
        scratch_shapes=[
            pltpu.VMEM((k, days), F32),
            pltpu.VMEM((half, days), F32),
            pltpu.VMEM((Y, days, share), F32),
            pltpu.SemaphoreType.DMA((Y + 1,)),
        ],
        cost_estimate=pl.CostEstimate(
            flops=6 * k * days * share * Y, bytes_accessed=4 * Y * share * (days + k), transcendentals=0
        ),
        compiler_params=pltpu.CompilerParams(vmem_limit_bytes=WIDE_LIMIT),
    )(core, pcs, field)


def first_kernel(recv_ref, sent_ref, loadings_ref, padded_ref):
    loadings = recv_ref[0] + recv_ref[1] + recv_ref[2] + recv_ref[3]
    k = loadings.shape[0]
    padded_ref[...] = jnp.zeros_like(padded_ref)
    padded_ref[0:k] = loadings
    loadings_ref[...] = loadings
    loadings = padded_ref[...]
    sent_ref[0:PAD] = rows_nt(loadings * loadings * loadings, loadings)
    sent_ref[PAD : 2 * PAD] = rows_nt(loadings, loadings)


def first(recv):
    k, share = recv.shape[1:]
    return pl.pallas_call(
        first_kernel,
        out_shape=(
            jax.ShapeDtypeStruct((2 * PAD, PAD), F32),
            jax.ShapeDtypeStruct((k, share), F32),
            jax.ShapeDtypeStruct((PAD, share), F32),
        ),
        in_specs=[VMEM],
        out_specs=(VMEM, VMEM, VMEM),
        compiler_params=pltpu.CompilerParams(vmem_limit_bytes=LIMIT),
    )(recv)


def second_kernel(cells, got_ref, loadings_ref, sent_ref, y_ref):
    corr = got_ref[PAD : 2 * PAD]
    rows = lax.broadcasted_iota(jnp.int32, corr.shape, 0)
    columns = lax.broadcasted_iota(jnp.int32, corr.shape, 1)
    colsq = jnp.sum(jnp.where(rows == columns, corr, 0.0), axis=1, keepdims=True)
    y = polar_rows(got_ref[0:PAD] - corr * colsq * (1.0 / cells))
    y_ref[...] = y
    sent_ref[...] = turn_cube(y, loadings_ref[...])


def next_y(cells, cube_ref, got_ref, y_ref):
    y = y_ref[...]
    cross = small_nn(y, got_ref[PAD : 2 * PAD])
    colsq = jnp.sum(y * cross, axis=1, keepdims=True)
    return polar_rows(cube_ref[...] - cross * colsq * (1.0 / cells))


def third_kernel(cells, cube_ref, got_ref, y_ref, loadings_ref, sent_ref, out_ref):
    y = next_y(cells, cube_ref, got_ref, y_ref)
    out_ref[...] = y
    sent_ref[...] = turn_cube(y, loadings_ref[...])


def last_kernel(cells, cube_ref, got_ref, y_ref, loadings_ref, terms_ref, rotated_ref, series_ref):
    k = rotated_ref.shape[0]
    y = next_y(cells, cube_ref, got_ref, y_ref)
    rotated_ref[...] = small_nn(y, loadings_ref[...])[0:k]
    parts = series_ref.shape[1] // PAD
    rows = terms_ref.shape[0] // parts
    for part in range(parts):
        terms = pad_rows(terms_ref[part * rows : (part + 1) * rows], PAD)
        series_ref[:, part * PAD : (part + 1) * PAD] = small_nn(y, terms)[0:k]


def whole(kernel, outs, *args):
    return pl.pallas_call(
        kernel,
        out_shape=tuple(jax.ShapeDtypeStruct(s, F32) for s in outs),
        in_specs=[VMEM] * len(args),
        out_specs=(VMEM,) * len(outs),
        compiler_params=pltpu.CompilerParams(vmem_limit_bytes=LIMIT),
    )(*args)


def terms_kernel(scale, where_ref, field_ref, near_ref, far_ref, out_ref):
    row, core = where_ref[0], where_ref[1]
    rows, share = near_ref.shape[1:]
    days = field_ref.shape[0]
    total = jnp.zeros((PAD, days), F32)
    for d in range(Y):
        group = CORE * lax.rem(row + Y - d, Y)
        for owner, loadings in ((core, near_ref[d]), (1 - core, far_ref[d])):
            lh, ll = split(pad_rows(loadings, PAD))
            high, low = split(columns(field_ref, group + owner, share))
            both = nt(jnp.concatenate([lh, ll], axis=0), high)
            total += both[0:PAD] + both[PAD : 2 * PAD] + nt(lh, low)
    for part in range(days // PAD):
        out_ref[part * rows : (part + 1) * rows] = total[0:rows, part * PAD : (part + 1) * PAD] * scale


def series_terms(field, near, far, where, scale):
    days = field.shape[0]
    rows, share = near.shape[1:]
    return pl.pallas_call(
        functools.partial(terms_kernel, scale),
        out_shape=jax.ShapeDtypeStruct((days // PAD * rows, PAD), F32),
        in_specs=[pl.BlockSpec(memory_space=pltpu.SMEM), VMEM, VMEM, VMEM],
        out_specs=VMEM,
        cost_estimate=pl.CostEstimate(
            flops=6 * days * PAD * share * Y * CORE,
            bytes_accessed=4 * Y * CORE * share * (days + rows),
            transcendentals=0,
        ),
        compiler_params=pltpu.CompilerParams(vmem_limit_bytes=LIMIT),
    )(where, field, near, far)


def swap(value, axes):
    return lax.all_to_all(value, axes, 0, 0)


def spread(value, count):
    return jnp.broadcast_to(value, (count,) + value.shape)


def on_device(field, pcs):
    k, days_here = pcs.shape
    groups = Y * CORE
    days_total = days_here * groups
    cells_total = field.shape[1] * Z * X
    share = field.shape[1] // groups
    core = lax.axis_index("core").astype(jnp.int32)
    row = lax.axis_index("y").astype(jnp.int32)

    scale = 1.0 / days_total**0.5
    theirs = lax.ppermute(parts(field, pcs, (1 - core)[None], scale), "core", [(0, 1), (1, 0)])
    recv = swap(theirs + parts(field, pcs, core[None], scale), "y")
    sent, narrow, loadings = first(recv)

    chunk = swap(sent.reshape(N_PLANE, 2 * ROWS, PAD), PLANE)
    near = [lax.ppermute(narrow, "y", [(i, (i + d) % Y) for i in range(Y)]) for d in range(1, Y)]
    chunk = swap(spread(jnp.sum(chunk, axis=0), Z), "z")
    base = swap(spread(jnp.sum(chunk, axis=0), N_PLANE), PLANE)
    base, near = lax.optimization_barrier((base, near))
    near = jnp.stack([narrow] + near)
    far = lax.ppermute(near, "core", [(0, 1), (1, 0)])
    base = base.reshape(2 * PAD, PAD)
    sent, y = whole(functools.partial(second_kernel, cells_total), [(PAD, PAD)] * 2, base, loadings)

    sent, near, far = lax.optimization_barrier((sent, near, far))
    terms = series_terms(field, near, far, jnp.stack([row, core]), days_total**0.5 / cells_total)
    chunk, terms = lax.optimization_barrier((swap(sent.reshape(N_PLANE, ROWS, PAD), PLANE), terms))
    chunk = jnp.sum(chunk, axis=0)
    width = ROWS * PAD
    both = jnp.concatenate([spread(chunk.reshape(1, width), Z), terms.reshape(Z, 1, -1)], axis=2)
    both = jnp.sum(swap(both, "z"), axis=0)
    got = swap(spread(both, N_PLANE), PLANE)
    cube = got[:, :, :width].reshape(PAD, PAD)
    terms = got[:, :, width:].reshape(X, groups, 1, -1)
    terms = jnp.sum(lax.dynamic_index_in_dim(terms, row * CORE + core, 1, keepdims=False), axis=0)
    sent, y = whole(
        functools.partial(third_kernel, cells_total), [(PAD, PAD)] * 2, cube, base, y, loadings
    )

    chunk = jnp.sum(swap(sent.reshape(N_PLANE, ROWS, PAD), PLANE), axis=0)
    got = swap(spread(jnp.concatenate([chunk.reshape(1, width), terms], axis=1), Z), "z")
    terms = got[:, :, width:].reshape(-1, PAD)
    chunk = jnp.sum(got[:, :, :width], axis=0).reshape(ROWS, PAD)
    chunk, terms = lax.optimization_barrier((chunk, terms))
    cube = swap(spread(chunk, N_PLANE), PLANE).reshape(PAD, PAD)
    return whole(
        functools.partial(last_kernel, cells_total),
        [(k, share), (k, days_here)],
        cube, base, y, loadings, terms,
    )


def solution(mesh):
    split_mesh = Mesh(mesh.devices.reshape(Z, X, Y, CORE), ("z", "x", "y", "core"))
    placed = (P(DAY, ("z", "x")), P(None, DAY))
    return jax.shard_map(
        on_device,
        mesh=split_mesh,
        in_specs=placed,
        out_specs=(P(None, ("z", "x", "y", "core")), P(None, DAY)),
        check_vma=False,
    )
```

```python
import functools

import jax
import jax.numpy as jnp
from jax import lax
from jax.experimental import pallas as pl
from jax.experimental.pallas import tpu as pltpu
from jax.sharding import Mesh, PartitionSpec as P

ITERS = 3
NS_STEPS = 12
Z, X, Y, CORE = 16, 4, 4, 2
PLANE = ("x", "y", "core")
DAY = ("y", "core")
PAD = 128
N_PLANE = X * Y * CORE
ROWS = PAD // N_PLANE
F32 = jnp.float32
VMEM = pl.BlockSpec(memory_space=pltpu.VMEM)
LIMIT = 24 << 20
FLOPS = 5000000000
WIDE_LIMIT = 52 << 20


def split(value):
    high = value.astype(jnp.bfloat16)
    return high, (value - high.astype(F32)).astype(jnp.bfloat16)


def nn(left, right):
    return jnp.dot(left, right, preferred_element_type=F32)


def nt(left, right):
    return lax.dot_general(left, right, (((1,), (1,)), ((), ())), preferred_element_type=F32)


def fold(value):
    half = value.shape[1] // 2
    return value[:, :half] + value[:, half:]


def pad_rows(value, rows):
    return jnp.concatenate([value, jnp.zeros((rows - value.shape[0], value.shape[1]), F32)], axis=0)


def small_nn(left, right):
    lh, ll = split(left)
    rh, rl = split(right)
    both = jnp.concatenate([rh, rl], axis=1)
    return fold(nn(jnp.concatenate([lh, ll], axis=1), jnp.concatenate([both, both], axis=0)))


def rows_nt(left, right):
    lh, ll = split(left)
    rh, rl = split(right)
    return fold(nt(lh, jnp.concatenate([rh, rl], axis=0))) + nt(ll, rh)


def polar_rows(grad):
    norm = jnp.sqrt(jnp.sum(jnp.sum(grad * grad, axis=1, keepdims=True), axis=0, keepdims=True))
    y = grad / (norm + 1e-06)
    for step in range(NS_STEPS):
        high, low = split(y)
        inner = fold(nt(high, jnp.concatenate([high, low], axis=0))) + nt(low, high)
        ih, il = split(inner)
        y = 1.5 * y - 0.5 * (fold(nn(ih, jnp.concatenate([high, low], axis=1))) + nn(il, high))
    return y


def turn_cube(y, loadings):
    turned = small_nn(y, loadings)
    return rows_nt(turned * turned * turned, loadings)


def columns(field_ref, group, share):
    return field_ref[:, pl.ds(pl.multiple_of(group * share, share), share)]


def parts_kernel(scale, core_ref, pcs_ref, field_ref, out_ref, pcs, wide, field, sems):
    share = out_ref.shape[2]
    copies = [pltpu.make_async_copy(pcs_ref, pcs, sems.at[Y])]
    for g in range(Y):
        start = pl.multiple_of((CORE * g + core_ref[0]) * share, share)
        copies.append(pltpu.make_async_copy(field_ref.at[:, pl.ds(start, share)], field.at[g], sems.at[g]))
    for copy in copies:
        copy.start()
    wide[...] = jnp.zeros_like(wide)
    copies[0].wait()
    wide[0 : pcs.shape[0]] = pcs[...] * scale
    half = wide.shape[0]
    left_high, left_low = split(wide[...])
    left = jnp.concatenate([left_high, left_low], axis=0)
    for g in range(Y):
        copies[1 + g].wait()
        high, low = split(field[g])
        both = nn(left, high)
        total = both[0:half] + both[half : 2 * half] + nn(left_high, low)
        out_ref[g] = total[0 : out_ref.shape[1]]


def parts(field, pcs, core, scale):
    k, days = pcs.shape
    share = field.shape[1] // (Y * CORE)
    half = (k + 15) // 16 * 16
    rows = (k + 7) // 8 * 8
    far = pl.BlockSpec(memory_space=pl.ANY)
    return pl.pallas_call(
        functools.partial(parts_kernel, scale),
        out_shape=jax.ShapeDtypeStruct((Y, rows, share), F32),
        in_specs=[pl.BlockSpec(memory_space=pltpu.SMEM), far, far],
        out_specs=VMEM,
        scratch_shapes=[
            pltpu.VMEM((k, days), F32),
            pltpu.VMEM((half, days), F32),
            pltpu.VMEM((Y, days, share), F32),
            pltpu.SemaphoreType.DMA((Y + 1,)),
        ],
        cost_estimate=pl.CostEstimate(
            flops=6 * k * days * share * Y, bytes_accessed=4 * Y * share * (days + k), transcendentals=0
        ),
        compiler_params=pltpu.CompilerParams(vmem_limit_bytes=WIDE_LIMIT),
    )(core, pcs, field)


def first_kernel(recv_ref, sent_ref, loadings_ref, padded_ref):
    loadings = recv_ref[0] + recv_ref[1] + recv_ref[2] + recv_ref[3]
    k = loadings.shape[0]
    padded_ref[...] = jnp.zeros_like(padded_ref)
    padded_ref[0:k] = loadings
    loadings_ref[...] = loadings
    loadings = padded_ref[...]
    sent_ref[0:PAD] = rows_nt(loadings * loadings * loadings, loadings)
    sent_ref[PAD : 2 * PAD] = rows_nt(loadings, loadings)


def first(recv):
    k, share = recv.shape[1:]
    return pl.pallas_call(
        first_kernel,
        out_shape=(
            jax.ShapeDtypeStruct((2 * PAD, PAD), F32),
            jax.ShapeDtypeStruct((k, share), F32),
            jax.ShapeDtypeStruct((PAD, share), F32),
        ),
        in_specs=[VMEM],
        out_specs=(VMEM, VMEM, VMEM),
        compiler_params=pltpu.CompilerParams(vmem_limit_bytes=LIMIT),
    )(recv)


def second_kernel(cells, got_ref, loadings_ref, sent_ref, y_ref):
    corr = got_ref[PAD : 2 * PAD]
    rows = lax.broadcasted_iota(jnp.int32, corr.shape, 0)
    columns = lax.broadcasted_iota(jnp.int32, corr.shape, 1)
    colsq = jnp.sum(jnp.where(rows == columns, corr, 0.0), axis=1, keepdims=True)
    y = polar_rows(got_ref[0:PAD] - corr * colsq * (1.0 / cells))
    y_ref[...] = y
    sent_ref[...] = turn_cube(y, loadings_ref[...])


def next_y(cells, cube_ref, got_ref, y_ref):
    y = y_ref[...]
    cross = small_nn(y, got_ref[PAD : 2 * PAD])
    colsq = jnp.sum(y * cross, axis=1, keepdims=True)
    return polar_rows(cube_ref[...] - cross * colsq * (1.0 / cells))


def third_kernel(cells, cube_ref, got_ref, y_ref, loadings_ref, sent_ref, out_ref):
    y = next_y(cells, cube_ref, got_ref, y_ref)
    out_ref[...] = y
    sent_ref[...] = turn_cube(y, loadings_ref[...])


def last_kernel(cells, cube_ref, got_ref, y_ref, loadings_ref, terms_ref, rotated_ref, series_ref):
    k = rotated_ref.shape[0]
    y = next_y(cells, cube_ref, got_ref, y_ref)
    rotated_ref[...] = small_nn(y, loadings_ref[...])[0:k]
    parts = series_ref.shape[1] // PAD
    rows = terms_ref.shape[0] // parts
    for part in range(parts):
        terms = pad_rows(terms_ref[part * rows : (part + 1) * rows], PAD)
        series_ref[:, part * PAD : (part + 1) * PAD] = small_nn(y, terms)[0:k]


def whole(kernel, outs, *args):
    return pl.pallas_call(
        kernel,
        out_shape=tuple(jax.ShapeDtypeStruct(s, F32) for s in outs),
        in_specs=[VMEM] * len(args),
        out_specs=(VMEM,) * len(outs),
        cost_estimate=pl.CostEstimate(flops=FLOPS, bytes_accessed=0, transcendentals=0),
        compiler_params=pltpu.CompilerParams(vmem_limit_bytes=LIMIT),
    )(*args)


def terms_kernel(scale, where_ref, field_ref, near_ref, far_ref, out_ref):
    row, core = where_ref[0], where_ref[1]
    rows, share = near_ref.shape[1:]
    days = field_ref.shape[0]
    total = jnp.zeros((PAD, days), F32)
    for d in range(Y):
        group = CORE * lax.rem(row + Y - d, Y)
        for owner, loadings in ((core, near_ref[d]), (1 - core, far_ref[d])):
            lh, ll = split(pad_rows(loadings, PAD))
            high, low = split(columns(field_ref, group + owner, share))
            both = nt(jnp.concatenate([lh, ll], axis=0), high)
            total += both[0:PAD] + both[PAD : 2 * PAD] + nt(lh, low)
    for part in range(days // PAD):
        out_ref[part * rows : (part + 1) * rows] = total[0:rows, part * PAD : (part + 1) * PAD] * scale


def series_terms(field, near, far, where, scale):
    days = field.shape[0]
    rows, share = near.shape[1:]
    return pl.pallas_call(
        functools.partial(terms_kernel, scale),
        out_shape=jax.ShapeDtypeStruct((days // PAD * rows, PAD), F32),
        in_specs=[pl.BlockSpec(memory_space=pltpu.SMEM), VMEM, VMEM, VMEM],
        out_specs=VMEM,
        cost_estimate=pl.CostEstimate(
            flops=6 * days * PAD * share * Y * CORE,
            bytes_accessed=4 * Y * CORE * share * (days + rows),
            transcendentals=0,
        ),
        compiler_params=pltpu.CompilerParams(vmem_limit_bytes=LIMIT),
    )(where, field, near, far)


def swap(value, axes):
    return lax.all_to_all(value, axes, 0, 0)


def spread(value, count):
    return jnp.broadcast_to(value, (count,) + value.shape)


def on_device(field, pcs):
    k, days_here = pcs.shape
    groups = Y * CORE
    days_total = days_here * groups
    cells_total = field.shape[1] * Z * X
    share = field.shape[1] // groups
    core = lax.axis_index("core").astype(jnp.int32)
    row = lax.axis_index("y").astype(jnp.int32)

    scale = 1.0 / days_total**0.5
    theirs = lax.ppermute(parts(field, pcs, (1 - core)[None], scale), "core", [(0, 1), (1, 0)])
    recv = swap(theirs + parts(field, pcs, core[None], scale), "y")
    sent, narrow, loadings = first(recv)

    chunk = swap(sent.reshape(N_PLANE, 2 * ROWS, PAD), PLANE)
    up = [(i, (i + 1) % Y) for i in range(Y)]
    first_up = lax.ppermute(narrow, "y", up)
    down = lax.ppermute(narrow, "y", [(j, i) for i, j in up])
    second_up = lax.ppermute(first_up, "y", up)
    chunk = swap(spread(jnp.sum(chunk, axis=0), Z), "z")
    base = swap(spread(jnp.sum(chunk, axis=0), N_PLANE), PLANE)
    base, down = lax.optimization_barrier((base, down))
    base = base.reshape(2 * PAD, PAD)
    sent, y = whole(functools.partial(second_kernel, cells_total), [(PAD, PAD)] * 2, base, loadings)

    sent, second_up = lax.optimization_barrier((sent, second_up))
    near = jnp.stack([narrow, first_up, second_up, down])
    far = lax.ppermute(near, "core", [(0, 1), (1, 0)])
    terms = series_terms(field, near, far, jnp.stack([row, core]), days_total**0.5 / cells_total)
    chunk, terms = lax.optimization_barrier((swap(sent.reshape(N_PLANE, ROWS, PAD), PLANE), terms))
    chunk = jnp.sum(chunk, axis=0)
    width = ROWS * PAD
    both = jnp.concatenate([spread(chunk.reshape(1, width), Z), terms.reshape(Z, 1, -1)], axis=2)
    both = jnp.sum(swap(both, "z"), axis=0)
    got = swap(spread(both, N_PLANE), PLANE)
    cube = got[:, :, :width].reshape(PAD, PAD)
    terms = got[:, :, width:].reshape(X, groups, 1, -1)
    terms = jnp.sum(lax.dynamic_index_in_dim(terms, row * CORE + core, 1, keepdims=False), axis=0)
    sent, y = whole(
        functools.partial(third_kernel, cells_total), [(PAD, PAD)] * 2, cube, base, y, loadings
    )

    chunk = jnp.sum(swap(sent.reshape(N_PLANE, ROWS, PAD), PLANE), axis=0)
    got = swap(spread(jnp.concatenate([chunk.reshape(1, width), terms], axis=1), Z), "z")
    terms = got[:, :, width:].reshape(-1, PAD)
    chunk = jnp.sum(got[:, :, :width], axis=0).reshape(ROWS, PAD)
    chunk, terms = lax.optimization_barrier((chunk, terms))
    cube = swap(spread(chunk, N_PLANE), PLANE).reshape(PAD, PAD)
    return whole(
        functools.partial(last_kernel, cells_total),
        [(k, share), (k, days_here)],
        cube, base, y, loadings, terms,
    )


def solution(mesh):
    split_mesh = Mesh(mesh.devices.reshape(Z, X, Y, CORE), ("z", "x", "y", "core"))
    placed = (P(DAY, ("z", "x")), P(None, DAY))
    return jax.shard_map(
        on_device,
        mesh=split_mesh,
        in_specs=placed,
        out_specs=(P(None, ("z", "x", "y", "core")), P(None, DAY)),
        check_vma=False,
    )
```

```python
import functools

import jax
import jax.numpy as jnp
from jax import lax
from jax.experimental import pallas as pl
from jax.experimental.pallas import tpu as pltpu
from jax.sharding import Mesh, PartitionSpec as P

ITERS = 3
NS_STEPS = 12
Z, X, Y, CORE = 16, 4, 4, 2
PLANE = ("x", "y", "core")
DAY = ("y", "core")
PAD = 128
N_PLANE = X * Y * CORE
ROWS = PAD // N_PLANE
F32 = jnp.float32
VMEM = pl.BlockSpec(memory_space=pltpu.VMEM)
LIMIT = 24 << 20
FLOPS = 10000000000
WIDE_LIMIT = 52 << 20


def split(value):
    high = value.astype(jnp.bfloat16)
    return high, (value - high.astype(F32)).astype(jnp.bfloat16)


def nn(left, right):
    return jnp.dot(left, right, preferred_element_type=F32)


def nt(left, right):
    return lax.dot_general(left, right, (((1,), (1,)), ((), ())), preferred_element_type=F32)


def fold(value):
    half = value.shape[1] // 2
    return value[:, :half] + value[:, half:]


def pad_rows(value, rows):
    return jnp.concatenate([value, jnp.zeros((rows - value.shape[0], value.shape[1]), F32)], axis=0)


def small_nn(left, right):
    lh, ll = split(left)
    rh, rl = split(right)
    both = jnp.concatenate([rh, rl], axis=1)
    return fold(nn(jnp.concatenate([lh, ll], axis=1), jnp.concatenate([both, both], axis=0)))


def rows_nt(left, right):
    lh, ll = split(left)
    rh, rl = split(right)
    return fold(nt(lh, jnp.concatenate([rh, rl], axis=0))) + nt(ll, rh)


def polar_rows(grad):
    norm = jnp.sqrt(jnp.sum(jnp.sum(grad * grad, axis=1, keepdims=True), axis=0, keepdims=True))
    y = grad / (norm + 1e-06)
    for step in range(NS_STEPS):
        high, low = split(y)
        inner = fold(nt(high, jnp.concatenate([high, low], axis=0))) + nt(low, high)
        ih, il = split(inner)
        y = 1.5 * y - 0.5 * (fold(nn(ih, jnp.concatenate([high, low], axis=1))) + nn(il, high))
    return y


def turn_cube(y, loadings):
    turned = small_nn(y, loadings)
    return rows_nt(turned * turned * turned, loadings)


def columns(field_ref, group, share):
    return field_ref[:, pl.ds(pl.multiple_of(group * share, share), share)]


def parts_kernel(scale, core_ref, pcs_ref, field_ref, out_ref, pcs, wide, field, sems):
    share = out_ref.shape[2]
    copies = [pltpu.make_async_copy(pcs_ref, pcs, sems.at[Y])]
    for g in range(Y):
        start = pl.multiple_of((CORE * g + core_ref[0]) * share, share)
        copies.append(pltpu.make_async_copy(field_ref.at[:, pl.ds(start, share)], field.at[g], sems.at[g]))
    for copy in copies:
        copy.start()
    wide[...] = jnp.zeros_like(wide)
    copies[0].wait()
    wide[0 : pcs.shape[0]] = pcs[...] * scale
    half = wide.shape[0]
    left_high, left_low = split(wide[...])
    left = jnp.concatenate([left_high, left_low], axis=0)
    for g in range(Y):
        copies[1 + g].wait()
        high, low = split(field[g])
        both = nn(left, high)
        total = both[0:half] + both[half : 2 * half] + nn(left_high, low)
        out_ref[g] = total[0 : out_ref.shape[1]]


def parts(field, pcs, core, scale):
    k, days = pcs.shape
    share = field.shape[1] // (Y * CORE)
    half = (k + 15) // 16 * 16
    rows = (k + 7) // 8 * 8
    far = pl.BlockSpec(memory_space=pl.ANY)
    return pl.pallas_call(
        functools.partial(parts_kernel, scale),
        out_shape=jax.ShapeDtypeStruct((Y, rows, share), F32),
        in_specs=[pl.BlockSpec(memory_space=pltpu.SMEM), far, far],
        out_specs=VMEM,
        scratch_shapes=[
            pltpu.VMEM((k, days), F32),
            pltpu.VMEM((half, days), F32),
            pltpu.VMEM((Y, days, share), F32),
            pltpu.SemaphoreType.DMA((Y + 1,)),
        ],
        cost_estimate=pl.CostEstimate(
            flops=6 * k * days * share * Y, bytes_accessed=4 * Y * share * (days + k), transcendentals=0
        ),
        compiler_params=pltpu.CompilerParams(vmem_limit_bytes=WIDE_LIMIT),
    )(core, pcs, field)


def first_kernel(recv_ref, sent_ref, loadings_ref, padded_ref):
    loadings = recv_ref[0] + recv_ref[1] + recv_ref[2] + recv_ref[3]
    k = loadings.shape[0]
    padded_ref[...] = jnp.zeros_like(padded_ref)
    padded_ref[0:k] = loadings
    loadings_ref[...] = loadings
    loadings = padded_ref[...]
    sent_ref[0:PAD] = rows_nt(loadings * loadings * loadings, loadings)
    sent_ref[PAD : 2 * PAD] = rows_nt(loadings, loadings)


def first(recv):
    k, share = recv.shape[1:]
    return pl.pallas_call(
        first_kernel,
        out_shape=(
            jax.ShapeDtypeStruct((2 * PAD, PAD), F32),
            jax.ShapeDtypeStruct((k, share), F32),
            jax.ShapeDtypeStruct((PAD, share), F32),
        ),
        in_specs=[VMEM],
        out_specs=(VMEM, VMEM, VMEM),
        compiler_params=pltpu.CompilerParams(vmem_limit_bytes=LIMIT),
    )(recv)


def second_kernel(cells, got_ref, loadings_ref, sent_ref, y_ref):
    corr = got_ref[PAD : 2 * PAD]
    rows = lax.broadcasted_iota(jnp.int32, corr.shape, 0)
    columns = lax.broadcasted_iota(jnp.int32, corr.shape, 1)
    colsq = jnp.sum(jnp.where(rows == columns, corr, 0.0), axis=1, keepdims=True)
    y = polar_rows(got_ref[0:PAD] - corr * colsq * (1.0 / cells))
    y_ref[...] = y
    sent_ref[...] = turn_cube(y, loadings_ref[...])


def next_y(cells, cube_ref, got_ref, y_ref):
    y = y_ref[...]
    cross = small_nn(y, got_ref[PAD : 2 * PAD])
    colsq = jnp.sum(y * cross, axis=1, keepdims=True)
    return polar_rows(cube_ref[...] - cross * colsq * (1.0 / cells))


def third_kernel(cells, cube_ref, got_ref, y_ref, loadings_ref, sent_ref, out_ref):
    y = next_y(cells, cube_ref, got_ref, y_ref)
    out_ref[...] = y
    sent_ref[...] = turn_cube(y, loadings_ref[...])


def last_kernel(cells, cube_ref, got_ref, y_ref, loadings_ref, terms_ref, rotated_ref, series_ref):
    k = rotated_ref.shape[0]
    y = next_y(cells, cube_ref, got_ref, y_ref)
    rotated_ref[...] = small_nn(y, loadings_ref[...])[0:k]
    parts = series_ref.shape[1] // PAD
    rows = terms_ref.shape[0] // parts
    for part in range(parts):
        terms = pad_rows(terms_ref[part * rows : (part + 1) * rows], PAD)
        series_ref[:, part * PAD : (part + 1) * PAD] = small_nn(y, terms)[0:k]


def whole(kernel, outs, *args):
    return pl.pallas_call(
        kernel,
        out_shape=tuple(jax.ShapeDtypeStruct(s, F32) for s in outs),
        in_specs=[VMEM] * len(args),
        out_specs=(VMEM,) * len(outs),
        cost_estimate=pl.CostEstimate(flops=FLOPS, bytes_accessed=0, transcendentals=0),
        compiler_params=pltpu.CompilerParams(vmem_limit_bytes=LIMIT),
    )(*args)


def terms_kernel(scale, where_ref, field_ref, near_ref, far_ref, out_ref):
    row, core = where_ref[0], where_ref[1]
    rows, share = near_ref.shape[1:]
    days = field_ref.shape[0]
    total = jnp.zeros((PAD, days), F32)
    for d in range(Y):
        group = CORE * lax.rem(row + Y - d, Y)
        for owner, loadings in ((core, near_ref[d]), (1 - core, far_ref[d])):
            lh, ll = split(pad_rows(loadings, PAD))
            high, low = split(columns(field_ref, group + owner, share))
            both = nt(jnp.concatenate([lh, ll], axis=0), high)
            total += both[0:PAD] + both[PAD : 2 * PAD] + nt(lh, low)
    for part in range(days // PAD):
        out_ref[part * rows : (part + 1) * rows] = total[0:rows, part * PAD : (part + 1) * PAD] * scale


def series_terms(field, near, far, where, scale):
    days = field.shape[0]
    rows, share = near.shape[1:]
    return pl.pallas_call(
        functools.partial(terms_kernel, scale),
        out_shape=jax.ShapeDtypeStruct((days // PAD * rows, PAD), F32),
        in_specs=[pl.BlockSpec(memory_space=pltpu.SMEM), VMEM, VMEM, VMEM],
        out_specs=VMEM,
        cost_estimate=pl.CostEstimate(
            flops=6 * days * PAD * share * Y * CORE,
            bytes_accessed=4 * Y * CORE * share * (days + rows),
            transcendentals=0,
        ),
        compiler_params=pltpu.CompilerParams(vmem_limit_bytes=LIMIT),
    )(where, field, near, far)


def swap(value, axes):
    return lax.all_to_all(value, axes, 0, 0)


def spread(value, count):
    return jnp.broadcast_to(value, (count,) + value.shape)


def on_device(field, pcs):
    k, days_here = pcs.shape
    groups = Y * CORE
    days_total = days_here * groups
    cells_total = field.shape[1] * Z * X
    share = field.shape[1] // groups
    core = lax.axis_index("core").astype(jnp.int32)
    row = lax.axis_index("y").astype(jnp.int32)

    scale = 1.0 / days_total**0.5
    theirs = lax.ppermute(parts(field, pcs, (1 - core)[None], scale), "core", [(0, 1), (1, 0)])
    recv = swap(theirs + parts(field, pcs, core[None], scale), "y")
    sent, narrow, loadings = first(recv)

    chunk = swap(sent.reshape(N_PLANE, 2 * ROWS, PAD), PLANE)
    up = [(i, (i + 1) % Y) for i in range(Y)]
    first_up = lax.ppermute(narrow, "y", up)
    down = lax.ppermute(narrow, "y", [(j, i) for i, j in up])
    second_up = lax.ppermute(first_up, "y", up)
    chunk = swap(spread(jnp.sum(chunk, axis=0), Z), "z")
    base = swap(spread(jnp.sum(chunk, axis=0), N_PLANE), PLANE)
    near = jnp.stack([narrow, first_up, second_up, down])
    far = lax.ppermute(near, "core", [(0, 1), (1, 0)])
    base = base.reshape(2 * PAD, PAD)
    sent, y = whole(functools.partial(second_kernel, cells_total), [(PAD, PAD)] * 2, base, loadings)

    sent, near, far = lax.optimization_barrier((sent, near, far))
    terms = series_terms(field, near, far, jnp.stack([row, core]), days_total**0.5 / cells_total)
    chunk, terms = lax.optimization_barrier((swap(sent.reshape(N_PLANE, ROWS, PAD), PLANE), terms))
    chunk = jnp.sum(chunk, axis=0)
    width = ROWS * PAD
    both = jnp.concatenate([spread(chunk.reshape(1, width), Z), terms.reshape(Z, 1, -1)], axis=2)
    both = jnp.sum(swap(both, "z"), axis=0)
    got = swap(spread(both, N_PLANE), PLANE)
    cube = got[:, :, :width].reshape(PAD, PAD)
    terms = got[:, :, width:].reshape(X, groups, 1, -1)
    terms = jnp.sum(lax.dynamic_index_in_dim(terms, row * CORE + core, 1, keepdims=False), axis=0)
    sent, y = whole(
        functools.partial(third_kernel, cells_total), [(PAD, PAD)] * 2, cube, base, y, loadings
    )

    chunk = jnp.sum(swap(sent.reshape(N_PLANE, ROWS, PAD), PLANE), axis=0)
    got = swap(spread(jnp.concatenate([chunk.reshape(1, width), terms], axis=1), Z), "z")
    terms = got[:, :, width:].reshape(-1, PAD)
    chunk = jnp.sum(got[:, :, :width], axis=0).reshape(ROWS, PAD)
    chunk, terms = lax.optimization_barrier((chunk, terms))
    cube = swap(spread(chunk, N_PLANE), PLANE).reshape(PAD, PAD)
    return whole(
        functools.partial(last_kernel, cells_total),
        [(k, share), (k, days_here)],
        cube, base, y, loadings, terms,
    )


def solution(mesh):
    split_mesh = Mesh(mesh.devices.reshape(Z, X, Y, CORE), ("z", "x", "y", "core"))
    placed = (P(DAY, ("z", "x")), P(None, DAY))
    return jax.shard_map(
        on_device,
        mesh=split_mesh,
        in_specs=placed,
        out_specs=(P(None, ("z", "x", "y", "core")), P(None, DAY)),
        check_vma=False,
    )
```
